256 devices in a mesh: tm: 16 (over y, x), height: 8 (over z), head: 2 (over core).
Axes of the slice: x: 4, y: 4, z: 8, core: 2. Of those that a mesh axis runs over, the one named last changes fastest.
Arguments:
- video_q: bfloat16 [128, 32, 8, 1536], P('tm', 'height', None, 'head'), may hold values from -41 to 41
- video_kv: bfloat16 [2, 128, 32, 8, 1536], P(None, 'tm', 'height', None, 'head'), may hold values from -4.5 to 4.5
- text_q: bfloat16 [256, 1536], P(None, 'head'), may hold values from -41 to 41
- text_k: bfloat16 [256, 1536], P(None, 'head'), may hold values from -4.5 to 4.5
- text_v: bfloat16 [256, 1536], P(None, 'head'), may hold values from -4.5 to 4.5
- tile_mask: int32 [32, 8, 2, 27], P('tm', 'height'), may hold values 0 or 1
- text_valid: int32 [256], replicated, may hold values 0 or 1
- w_out: bfloat16 [1536, 3072], P('head', 'height'), may hold values from -0.15625 to 0.15625
Outputs:
- video_out: bfloat16 [128, 32, 8, 3072], P('tm', 'height', None, 'head')
- text_out: bfloat16 [256, 3072], P(None, 'head')
The draws below stay inside these ranges and needn't reach their ends.
All inputs are finite; a program needn't handle non-finite values. No bound on the sum of `tile_mask` on one device may be relied on, other than what follows from the above.
Results may differ from the reference program's by a relative error of at most 0.023.
Values may be sent and summed in bfloat16 or wider, within the bound.
No kernel may reach another device: no remote copies, remote signals or barrier semaphores. Data moves between devices by JAX's collectives and lax.ppermute only.
A program may use at most 64 MiB of HBM per device.

```python
import jax
import jax.numpy as jnp
from jax import lax

D = 3072
HEADS = 12
HEAD_DIM = 128
TILE = 4
TEXT = 256
WT = 2
FRAMES = 128
ROWS = 32
COLS = 8
HD = 1536


def normal_keys(key):
    return jnp.clip(jax.random.normal(key, (FRAMES, ROWS, COLS, HD), jnp.float32), -4.5, 4.5)


def draw_video_kv(key, part):
    base_key = key
    key = jax.random.fold_in(key, 1)
    key_part = normal_keys(base_key)
    value_part = jnp.clip(jax.random.normal(jax.random.fold_in(key, 3), key_part.shape, jnp.float32), -4.5, 4.5)
    return jnp.stack([key_part, value_part], axis=0).astype(jnp.bfloat16)


def draw_video_q(key, part):
    key = jax.random.fold_in(key, 5)
    result = 2.0 * jnp.clip(jax.random.normal(jax.random.fold_in(key, 1), (FRAMES, ROWS, COLS, HD), jnp.float32), -4.5, 4.5)
    return result.astype(jnp.bfloat16)


def draw_text_q(key, part):
    key = jax.random.fold_in(key, 7)
    result = 3.0 * jnp.clip(jax.random.normal(jax.random.fold_in(key, 1), (TEXT, HD), jnp.float32), -4.5, 4.5)
    return result.astype(jnp.bfloat16)


def plant(values, stream_key, low, high):
    index_at = [jax.random.randint(jax.random.fold_in(stream_key, axis), (), 0, length) for axis, length in enumerate(values.shape)]
    longest = values.shape.index(max(values.shape))
    beside = index_at[:longest] + [(index_at[longest] + 1) % values.shape[longest]] + index_at[longest + 1:]
    return values.at[tuple(index_at)].set(low).at[tuple(beside)].set(high)


def shard_levels(stream_key, dims, pieces, least, high):
    def one(axis_at, blocks):
        steps = jax.random.uniform(jax.random.fold_in(jax.random.fold_in(stream_key, 6), axis_at), (blocks,), jnp.float32, least / len(pieces), high / len(pieces))
        return jnp.repeat(jnp.exp(steps), dims[axis_at] // blocks).reshape((-1,) + (1,) * (len(dims) - axis_at - 1))

    gain = one(*pieces[0])
    for cut in pieces[1:]:
        gain = gain * one(*cut)
    return gain


def normal_values(stream_key, extent, deviation, bound, shards=(), held_as=jnp.bfloat16):
    drawn = deviation * jax.random.normal(stream_key, extent, jnp.float32)
    if shards:
        drawn = drawn * shard_levels(stream_key, extent, shards, -0.22, 0.18)
    return jnp.clip(drawn, -bound, bound).astype(held_as)


def setup_inputs(seed: int = 0) -> dict:
    arg_keys = jax.random.split(jax.random.key(seed), 9)
    video_q = draw_video_q(jax.random.fold_in(arg_keys[8], 71), 0)
    video_kv = draw_video_kv(jax.random.fold_in(arg_keys[8], 71), 0)
    text_q = draw_text_q(jax.random.fold_in(arg_keys[8], 71), 0)
    text_k = normal_values(arg_keys[3], (TEXT, HD), 1.0, 4.5, ((1, 2),))
    text_v = normal_values(arg_keys[4], (TEXT, HD), 1.0, 4.5, ((1, 2),))
    tile_mask = plant((jax.random.randint(arg_keys[5], (FRAMES // TILE, ROWS // TILE, WT, 27), 0, 4) < 3).astype(jnp.int32), jax.random.fold_in(arg_keys[5], 1), 0, 1)
    text_valid = plant((jax.random.randint(arg_keys[6], (TEXT,), 0, 4) < 3).astype(jnp.int32), jax.random.fold_in(arg_keys[6], 1), 0, 1)
    w_out = normal_values(arg_keys[7], (HD, D), HD ** -0.5, 0.15625, ((0, 2), (1, 8)))
    return dict(video_q=video_q, video_kv=video_kv, text_q=text_q, text_k=text_k, text_v=text_v, tile_mask=tile_mask, text_valid=text_valid, w_out=w_out)


def to_tiles(grid):
    frame_count, row_count, col_count, last_width = grid.shape
    tiled = grid.reshape(frame_count // TILE, TILE, row_count // TILE, TILE, col_count // TILE, TILE, last_width)
    tiled = tiled.transpose(0, 2, 4, 1, 3, 5, 6)
    return tiled.reshape(frame_count // TILE, row_count // TILE, col_count // TILE, TILE ** 3, last_width)


def from_tiles(tiled):
    tile_t, tile_h, tile_w, cube_count, last_width = tiled.shape
    grid = tiled.reshape(tile_t, tile_h, tile_w, TILE, TILE, TILE, last_width).transpose(0, 3, 1, 4, 2, 5, 6)
    return grid.reshape(tile_t * TILE, tile_h * TILE, tile_w * TILE, last_width)


def attend_rows(queries, key_rows, value_rows, allowed, head_count):
    q_count = queries.shape[0]
    k_count = key_rows.shape[0]
    head_width = queries.shape[1] // head_count
    q_split = queries.reshape(q_count, head_count, head_width).astype(jnp.float32)
    k_split = key_rows.reshape(k_count, head_count, head_width).astype(jnp.float32)
    v_split = value_rows.reshape(k_count, head_count, head_width).astype(jnp.float32)
    scores = jnp.einsum("qhd,khd->hqk", q_split, k_split) * (head_width ** -0.5)
    scores = jnp.where(allowed[None, None, :], scores, -jnp.inf)
    highest = jnp.max(scores, axis=-1, keepdims=True)
    weights = jnp.exp(scores - highest)
    totals = jnp.sum(weights, axis=-1)
    rounded = lax.optimization_barrier(weights.astype(jnp.bfloat16)).astype(jnp.float32)
    mixture = jnp.einsum("hqk,khd->qhd", rounded, v_split) / totals.T[:, :, None]
    return mixture.reshape(q_count, head_count * head_width).astype(jnp.bfloat16)


def reference(video_q, video_kv, text_q, text_k, text_v, tile_mask, text_valid, w_out):
    q_tiles = to_tiles(video_q)
    pad_spec = ((1, 1), (1, 1), (1, 1), (0, 0), (0, 0))
    k_tiles = jnp.pad(to_tiles(video_kv[0]), pad_spec)
    v_tiles = jnp.pad(to_tiles(video_kv[1]), pad_spec)
    tiles_t, tiles_h, tiles_w = q_tiles.shape[0], q_tiles.shape[1], q_tiles.shape[2]
    cube = TILE ** 3
    width_all = video_q.shape[3]
    offsets = jnp.arange(27, dtype=jnp.int32)
    step_t = offsets // 9
    step_h = (offsets // 3) % 3
    step_w = offsets % 3
    text_ok = text_valid > 0

    def one_tile(tile_a, tile_b, tile_c):
        start = (tile_a.astype(jnp.int32), tile_b.astype(jnp.int32), tile_c.astype(jnp.int32), jnp.int32(0), jnp.int32(0))
        key_win = lax.dynamic_slice(k_tiles, start, (3, 3, 3, cube, width_all)).reshape(27 * cube, width_all)
        val_win = lax.dynamic_slice(v_tiles, start, (3, 3, 3, cube, width_all)).reshape(27 * cube, width_all)
        inside = (tile_a + step_t - 1 >= 0) & (tile_a + step_t - 1 < tiles_t)
        inside = inside & (tile_b + step_h - 1 >= 0) & (tile_b + step_h - 1 < tiles_h)
        inside = inside & (tile_c + step_w - 1 >= 0) & (tile_c + step_w - 1 < tiles_w)
        chosen = ((tile_mask[tile_a, tile_b, tile_c] > 0) | (offsets == 13)) & inside
        allowed = jnp.concatenate([jnp.repeat(chosen, cube), text_ok])
        key_rows = jnp.concatenate([key_win, text_k], axis=0)
        value_rows = jnp.concatenate([val_win, text_v], axis=0)
        return attend_rows(q_tiles[tile_a, tile_b, tile_c], key_rows, value_rows, allowed, HEADS)

    col_ids = jnp.arange(tiles_w, dtype=jnp.int32)

    def one_pair(pair_id):
        tile_a = pair_id // tiles_h
        tile_b = pair_id % tiles_h
        return jax.vmap(lambda tile_c: one_tile(tile_a, tile_b, tile_c))(col_ids)

    outputs = lax.map(one_pair, jnp.arange(tiles_t * tiles_h, dtype=jnp.int32))
    outputs = outputs.reshape(tiles_t, tiles_h, tiles_w, cube, width_all)
    attended = from_tiles(outputs)
    frame_count, row_count, col_count = video_q.shape[0], video_q.shape[1], video_q.shape[2]
    video_out = jnp.dot(attended.reshape(-1, width_all), w_out, preferred_element_type=jnp.float32)
    video_out = video_out.astype(jnp.bfloat16).reshape(frame_count, row_count, col_count, -1)

    all_keys = jnp.concatenate([video_kv[0].reshape(-1, width_all), text_k], axis=0)
    all_values = jnp.concatenate([video_kv[1].reshape(-1, width_all), text_v], axis=0)
    all_allowed = jnp.concatenate([jnp.ones((frame_count * row_count * col_count,), bool), text_ok])

    def text_head(head_id):
        first_col = (head_id * HEAD_DIM).astype(jnp.int32)
        q_part = lax.dynamic_slice_in_dim(text_q, first_col, HEAD_DIM, 1)
        k_part = lax.dynamic_slice_in_dim(all_keys, first_col, HEAD_DIM, 1)
        v_part = lax.dynamic_slice_in_dim(all_values, first_col, HEAD_DIM, 1)
        return attend_rows(q_part, k_part, v_part, all_allowed, 1)

    per_head = lax.map(text_head, jnp.arange(HEADS, dtype=jnp.int32))
    text_attended = per_head.transpose(1, 0, 2).reshape(text_q.shape[0], width_all)
    text_out = jnp.dot(text_attended, w_out, preferred_element_type=jnp.float32).astype(jnp.bfloat16)
    return video_out, text_out
```

```python
import functools

import jax
import jax.numpy as jnp
from jax import lax
from jax.experimental import pallas as pl
from jax.experimental.pallas import tpu as pltpu
from jax.sharding import PartitionSpec as P

HEAD_DIM = 128
TILE = 4
HEADS_HERE = 6
PAIR = 128
OWN = 256
TEXT = 256
WIDTH = HEADS_HERE * HEAD_DIM
RANKS = 128
ROWS_EACH = HEADS_HERE * TEXT // RANKS
SLOT = 16
SCALE2 = HEAD_DIM ** (-0.5) * 1.4426950408889634
LOW = -1e30
BF = jnp.bfloat16
F32 = jnp.float32


def dot_t(a, b):
    return lax.dot_general(a, b, (((1,), (1,)), ((), ())), preferred_element_type=F32)


def dot(a, b):
    return jnp.dot(a, b, preferred_element_type=F32)


def text_part_kernel(pos, valid, tq, kv, tk, tv, out, acc_s, stat_s):
    head = pl.program_id(0)
    first = (pos[0] == 0) & (pos[1] == 0)
    q = tq[...]
    s_own = dot_t(q, kv[0]) * SCALE2
    bias = jnp.where((valid[...] > 0) & first, 0.0, LOW)
    s_text = dot_t(q, tk[...]) * SCALE2 + bias
    high = jnp.max(jnp.maximum(s_own, s_text), axis=1, keepdims=True)
    high = high.astype(BF).astype(F32)
    p_own = jnp.exp2(s_own - high)
    p_text = jnp.exp2(s_text - high)
    total = jnp.sum(p_own + p_text, axis=1, keepdims=True)
    acc = dot(p_own.astype(BF), kv[1]) + dot(p_text.astype(BF), tv[...])
    rows = pl.ds(pl.multiple_of(head * TEXT, TEXT), TEXT)
    acc_s[rows, :] = acc
    lane = lax.broadcasted_iota(jnp.int32, (TEXT, HEAD_DIM), 1)
    total_high = total.astype(BF).astype(F32)
    stat_s[rows, :] = jnp.where(
        lane < SLOT, high, jnp.where(lane < 2 * SLOT, total_high, total - total_high)
    )

    @pl.when(head == HEADS_HERE - 1)
    def _():
        row = lax.broadcasted_iota(jnp.int32, (SLOT, HEAD_DIM), 0)
        col = lax.broadcasted_iota(jnp.int32, (SLOT, HEAD_DIM), 1)
        same = (jnp.bitwise_and(col, SLOT - 1) == row) & (row < ROWS_EACH) & (col < 3 * SLOT)
        for rank in range(RANKS):
            start = rank * ROWS_EACH
            part = acc_s[start : start + SLOT, :]
            stat = stat_s[start : start + SLOT, :]
            stat_row = jnp.sum(jnp.where(same, stat, 0.0), axis=0, keepdims=True)
            full = jnp.where(row < ROWS_EACH, part, jnp.where(row == ROWS_EACH, stat_row, 0.0))
            out[rank] = full.astype(BF)


def text_part(pos, valid, tq, kv, tk, tv):
    col = lambda h, *_: (0, h)
    return pl.pallas_call(
        text_part_kernel,
        grid_spec=pltpu.PrefetchScalarGridSpec(
            num_scalar_prefetch=1,
            grid=(HEADS_HERE,),
            in_specs=[
                pl.BlockSpec((1, TEXT), lambda h, *_: (0, 0)),
                pl.BlockSpec((TEXT, HEAD_DIM), col),
                pl.BlockSpec((2, OWN, HEAD_DIM), lambda h, *_: (0, 0, h)),
                pl.BlockSpec((TEXT, HEAD_DIM), col),
                pl.BlockSpec((TEXT, HEAD_DIM), col),
            ],
            out_specs=pl.BlockSpec((RANKS, SLOT, HEAD_DIM), lambda h, *_: (0, 0, 0)),
            scratch_shapes=[
                pltpu.VMEM((HEADS_HERE * TEXT + SLOT, HEAD_DIM), F32),
                pltpu.VMEM((HEADS_HERE * TEXT + SLOT, HEAD_DIM), F32),
            ],
        ),
        out_shape=jax.ShapeDtypeStruct((RANKS, SLOT, HEAD_DIM), BF),
        compiler_params=pltpu.CompilerParams(vmem_limit_bytes=32 << 20),
        name="text_part",
    )(pos, valid, tq, kv, tk, tv)


def combine_kernel(parts, out):
    count = RANKS * SLOT
    data = parts[...].reshape(count, HEAD_DIM)
    sel_row = lax.broadcasted_iota(jnp.int32, (RANKS, count), 0)
    sel_col = lax.broadcasted_iota(jnp.int32, (RANKS, count), 1)
    pick = jnp.where(sel_col == sel_row * SLOT + ROWS_EACH, 1.0, 0.0).astype(BF)
    stats = dot(pick, data)
    high = jnp.max(stats, axis=0, keepdims=True)
    weight = jnp.exp2(stats - high)
    totals = pltpu.roll(stats, HEAD_DIM - SLOT, 1) + pltpu.roll(stats, HEAD_DIM - 2 * SLOT, 1)
    total = jnp.sum(weight * totals, axis=0, keepdims=True)
    lane = lax.broadcasted_iota(jnp.int32, (RANKS, HEAD_DIM), 1)
    weight = jnp.where(lane < ROWS_EACH, weight / total, 0.0)
    weight_high = weight.astype(BF)
    weight_low = (weight - weight_high.astype(F32)).astype(BF)
    ex_row = lax.broadcasted_iota(jnp.int32, (count, RANKS), 0)
    ex_col = lax.broadcasted_iota(jnp.int32, (count, RANKS), 1)
    spread = jnp.where(lax.shift_right_logical(ex_row, 4) == ex_col, 1.0, 0.0).astype(BF)
    diag = jnp.bitwise_and(ex_row, SLOT - 1) == ex_col
    total_rows = jnp.zeros((HEAD_DIM, HEAD_DIM), F32)
    for part in (weight_high, weight_low):
        grown = jnp.where(diag, dot(spread, part), 0.0).astype(BF)
        total_rows += lax.dot_general(
            grown, data, (((0,), (0,)), ((), ())), preferred_element_type=F32
        )
    done = total_rows[:SLOT].astype(BF)
    for rank in range(RANKS):
        out[rank] = done


def combine(parts):
    return pl.pallas_call(
        combine_kernel,
        out_shape=jax.ShapeDtypeStruct((RANKS, SLOT, HEAD_DIM), BF),
        compiler_params=pltpu.CompilerParams(vmem_limit_bytes=32 << 20),
        name="text_combine",
    )(parts)


def unpack_kernel(parts, out, flat):
    for rank in range(RANKS):
        start = rank * ROWS_EACH
        flat[start : start + ROWS_EACH, :] = parts[rank].astype(F32)[:ROWS_EACH]
    for head in range(HEADS_HERE):
        out[:, head * HEAD_DIM : (head + 1) * HEAD_DIM] = flat[
            head * TEXT : (head + 1) * TEXT, :
        ].astype(BF)


def unpack(parts):
    return pl.pallas_call(
        unpack_kernel,
        out_shape=jax.ShapeDtypeStruct((TEXT, WIDTH), BF),
        scratch_shapes=[pltpu.VMEM((HEADS_HERE * TEXT, HEAD_DIM), F32)],
        compiler_params=pltpu.CompilerParams(vmem_limit_bytes=32 << 20),
        name="text_unpack",
    )(parts)


def video_kernel(pos, mask, valid, q, tk, tv, own, *rest):
    chunks = rest[:10]
    out, bias_s = rest[10:]

    @pl.when(pl.program_id(0) == 0)
    def _():
        row = lax.broadcasted_iota(jnp.int32, (8, PAIR), 0)
        col = lax.broadcasted_iota(jnp.int32, (8, PAIR), 1)
        second_q = row >= TILE
        second_k = jnp.bitwise_and(col, 7) >= TILE
        for a in range(2):
            for i in range(3):
                for j in range(3):
                    where_t = pos[0] * 2 + a + i - 1
                    where_h = pos[1] + j - 1
                    inside = (where_t >= 0) & (where_t < pos[3]) & (where_h >= 0) & (where_h < pos[4])
                    base = 9 * i + 3 * j

                    def one(c, k):
                        if base + k == 13:
                            return jnp.where(inside, 0.0, LOW)
                        ok = inside & (mask[(a * 2 + c) * 27 + base + k] > 0)
                        return jnp.where(ok, 0.0, LOW)

                    low = jnp.where(second_k, one(0, 2), one(0, 1))
                    high = jnp.where(second_k, one(1, 1), one(1, 0))
                    bias_s[a, i, j] = jnp.where(second_q, high, low)

    text_bias = jnp.where(valid[...] > 0, 0.0, LOW)
    low_t, own_low, own_high, high_t = (
        [chunks[0], chunks[1], chunks[2]],
        [chunks[3], None, chunks[4]],
        [chunks[5], None, chunks[6]],
        [chunks[7], chunks[8], chunks[9]],
    )

    def load(ref, part, a):
        if ref is None:
            return own[part, a * PAIR : (a + 1) * PAIR, :]
        return ref[part]

    def rows(part):
        return (
            jnp.concatenate([load(r, part, 0) for r in low_t], axis=0),
            jnp.concatenate(
                [load(r, part, 0) for r in own_low] + [load(r, part, 1) for r in own_high],
                axis=0,
            ),
            jnp.concatenate([load(r, part, 0) for r in high_t], axis=0),
        )

    queries = q[...]
    k_low, k_mid, k_high = rows(0)
    v_low, v_mid, v_high = rows(1)
    s_mid = dot_t(queries, k_mid)
    s_text = dot_t(queries, tk[...])
    s_sides = (dot_t(queries[:PAIR], k_low), dot_t(queries[PAIR:], k_high))
    v_sides = (v_low, v_high)
    for a in range(2):
        mine = slice(a * PAIR, (a + 1) * PAIR)
        pieces = []
        for i in range(3):
            for j in range(3):
                at = (a + i - 1) * 3 + j
                if 0 <= a + i - 1 <= 1:
                    piece = s_mid[mine, at * PAIR : (at + 1) * PAIR]
                else:
                    piece = s_sides[a][:, j * PAIR : (j + 1) * PAIR]
                piece = piece.reshape(PAIR // 8, 8, PAIR) * SCALE2 + bias_s[a, i, j][None]
                pieces.append(piece.reshape(PAIR, PAIR))
        text_piece = s_text[mine] * SCALE2 + text_bias
        pieces.append(text_piece[:, :PAIR])
        pieces.append(text_piece[:, PAIR:])
        high = functools.reduce(jnp.maximum, pieces)
        high = jnp.max(high, axis=1, keepdims=True)
        weights = [jnp.exp2(piece - high) for piece in pieces]
        total = jnp.sum(functools.reduce(jnp.add, weights), axis=1, keepdims=True)
        weights = [w.astype(BF) for w in weights]
        side = weights[:3] if a == 0 else weights[6:9]
        mid = weights[3:9] if a == 0 else weights[:6]
        mixed = (
            dot(jnp.concatenate(side, axis=1), v_sides[a])
            + dot(jnp.concatenate(mid, axis=1), v_mid)
            + dot(jnp.concatenate(weights[9:], axis=1), tv[...])
        )
        out[mine, :] = (mixed / total).astype(BF)


def video_attention(pos, mask, valid, q, tk, tv, own, chunks):
    col = lambda h, *_: (0, h)
    col3 = lambda h, *_: (0, 0, h)
    return pl.pallas_call(
        video_kernel,
        grid_spec=pltpu.PrefetchScalarGridSpec(
            num_scalar_prefetch=2,
            grid=(HEADS_HERE,),
            in_specs=[
                pl.BlockSpec((1, TEXT), lambda h, *_: (0, 0)),
                pl.BlockSpec((OWN, HEAD_DIM), col),
                pl.BlockSpec((TEXT, HEAD_DIM), col),
                pl.BlockSpec((TEXT, HEAD_DIM), col),
                pl.BlockSpec((2, OWN, HEAD_DIM), col3),
            ]
            + [pl.BlockSpec((2, PAIR, HEAD_DIM), col3)] * 10,
            out_specs=pl.BlockSpec((OWN, HEAD_DIM), col),
            scratch_shapes=[pltpu.VMEM((2, 3, 3, 8, PAIR), F32)],
        ),
        out_shape=jax.ShapeDtypeStruct((OWN, WIDTH), BF),
        compiler_params=pltpu.CompilerParams(vmem_limit_bytes=40 << 20),
        name="video_attention",
    )(pos, mask, valid, q, tk, tv, own, *chunks)


def share_kernel(pos, rows, w, out):
    out[...] = dot(rows[...], w[...]).astype(BF)


def finish_kernel(pos, rows, w, other, out):
    out[...] = (dot(rows[...], w[...]) + other[...].astype(F32)).astype(BF)


def project(pos, rows, w_all, other):
    count = rows.shape[0]
    depth, width = w_all.shape[0] // 8, w_all.shape[1]
    if other is None:
        pick = lambda g, p: ((1 - p[2]) * 4 + g, 0)
    else:
        pick = lambda g, p: (p[2] * 4 + g, 0)
    specs = [
        pl.BlockSpec((count, WIDTH), lambda g, p: (0, 0)),
        pl.BlockSpec((depth, width), pick),
    ]
    args = [rows, w_all]
    if other is not None:
        specs.append(pl.BlockSpec((count, width), lambda g, p: (0, g)))
        args.append(other)
    return pl.pallas_call(
        share_kernel if other is None else finish_kernel,
        grid_spec=pltpu.PrefetchScalarGridSpec(
            num_scalar_prefetch=1,
            grid=(4,),
            in_specs=specs,
            out_specs=pl.BlockSpec((count, width), lambda g, p: (0, g)),
        ),
        out_shape=jax.ShapeDtypeStruct((count, 4 * width), BF),
        compiler_params=pltpu.CompilerParams(vmem_limit_bytes=32 << 20),
        name="project_share" if other is None else "project_finish",
    )(pos, *args)


def shards(video_q, video_kv, text_q, text_k, text_v, tile_mask, text_valid, w_out):
    frames, rows, cols, width = video_q.shape
    t_count, h_count = lax.axis_size("tm"), lax.axis_size("height")
    zero = jnp.int32(0)
    pos = jnp.stack(
        [
            lax.axis_index("tm"),
            lax.axis_index("height"),
            lax.axis_index("head"),
            zero + t_count * 2,
            zero + h_count,
        ]
    ).astype(jnp.int32)
    mask = tile_mask.reshape(-1)
    valid = text_valid.reshape(1, TEXT)
    own = video_kv.reshape(2, OWN, width)
    q = video_q.reshape(OWN, width)
    early, late = own[:, :PAIR], own[:, PAIR:]

    def up(x, axis, n):
        return lax.ppermute(x, axis, [(i, i + 1) for i in range(n - 1)])

    def down(x, axis, n):
        return lax.ppermute(x, axis, [(i + 1, i) for i in range(n - 1)])

    zl_late, zh_late = up(late, "height", h_count), down(late, "height", h_count)
    tm_low, tm_high = up(late, "tm", t_count), down(early, "tm", t_count)
    zl_early, zh_early = up(early, "height", h_count), down(early, "height", h_count)
    low_zl, low_zh = up(zl_late, "tm", t_count), up(zh_late, "tm", t_count)
    high_zl, high_zh = down(zl_early, "tm", t_count), down(zh_early, "tm", t_count)
    w_all = lax.all_gather(w_out, "height", axis=0, tiled=True)

    parts = text_part(pos, valid, text_q, own, text_k, text_v)
    parts = lax.all_to_all(parts, ("tm", "height"), 0, 0, tiled=True)
    parts = combine(parts)
    parts = lax.all_to_all(parts, ("tm", "height"), 0, 0, tiled=True)
    text_rows = unpack(parts)

    chunks = [low_zl, tm_low, low_zh, zl_early, zh_early, zl_late, zh_late, high_zl, tm_high, high_zh]
    video_rows = video_attention(pos, mask, valid, q, text_k, text_v, own, chunks)

    swap = [(0, 1), (1, 0)]
    video_share = lax.ppermute(project(pos, video_rows, w_all, None), "head", swap)
    text_share = lax.ppermute(project(pos, text_rows, w_all, None), "head", swap)
    video_out = project(pos, video_rows, w_all, video_share)
    text_out = project(pos, text_rows, w_all, text_share)
    return video_out.reshape(frames, rows, cols, -1), text_out


def solution(mesh):
    return jax.shard_map(
        shards,
        mesh=mesh,
        in_specs=(
            P("tm", "height", None, "head"),
            P(None, "tm", "height", None, "head"),
            P(None, "head"),
            P(None, "head"),
            P(None, "head"),
            P("tm", "height", None, None),
            P(),
            P("head", "height"),
        ),
        out_specs=(P("tm", "height", None, "head"), P(None, "head")),
        check_vma=False,
    )
```

```python
import functools

import jax
import jax.numpy as jnp
from jax import lax
from jax.experimental import pallas as pl
from jax.experimental.pallas import tpu as pltpu
from jax.sharding import PartitionSpec as P

HEAD_DIM = 128
TILE = 4
HEADS_HERE = 6
PAIR = 128
OWN = 256
TEXT = 256
WIDTH = HEADS_HERE * HEAD_DIM
PLANE = 16
EACH = HEADS_HERE * TEXT // PLANE
SLOT = 112
SCALE2 = HEAD_DIM ** (-0.5) * 1.4426950408889634
LOW = -1e30
VMEM = 60 << 20
BF = jnp.bfloat16
F32 = jnp.float32


def dot_t(a, b):
    return lax.dot_general(a, b, (((1,), (1,)), ((), ())), preferred_element_type=F32)


def dot(a, b):
    return jnp.dot(a, b, preferred_element_type=F32)


def fetch(pairs, sems, columns):
    copies = []
    for at, (source, target) in enumerate(pairs):
        where = (slice(None),) * (len(source.shape) - 1) + (columns,)
        copies.append(pltpu.make_async_copy(source.at[where], target.at[where], sems.at[at]))
    for copy in copies:
        copy.start()
    return copies


def wait_all(copies):
    for copy in copies:
        copy.wait()


FIRST, REST = slice(0, HEAD_DIM), slice(HEAD_DIM, WIDTH)


def stat_rows(values):
    row = lax.broadcasted_iota(jnp.int32, (EACH, HEAD_DIM), 0)
    col = lax.broadcasted_iota(jnp.int32, (EACH, HEAD_DIM), 1)
    lines = [jnp.sum(jnp.where(row == col, v, 0.0), axis=0, keepdims=True) for v in values]
    return lay_out(lines)


def lay_out(lines):
    row = lax.broadcasted_iota(jnp.int32, (SLOT - EACH, HEAD_DIM), 0)
    full = jnp.zeros((SLOT - EACH, HEAD_DIM), F32)
    for at, line in enumerate(lines):
        full = jnp.where(row == at, line, full)
    return full.astype(BF)


def split(total):
    high = total.astype(BF).astype(F32)
    return high, total - high


def text_part_kernel(
    pos, valid, tq_h, kv_h, tk_h, tv_h, out, tq, kv, tk, tv, acc_s, high_s, total_s, sems
):
    pairs = [(tq_h, tq), (kv_h, kv), (tk_h, tk), (tv_h, tv)]
    begun = fetch(pairs, sems.at[0], FIRST)
    later = fetch(pairs, sems.at[1], REST)
    first = (pos[0] == 0) & (pos[1] == 0)
    bias = jnp.where((valid[...] > 0) & first, 0.0, LOW)
    for head in range(HEADS_HERE):
        if head == 0:
            wait_all(begun)
        elif head == 1:
            wait_all(later)
        cols = slice(head * HEAD_DIM, (head + 1) * HEAD_DIM)
        q = tq[:, cols]
        s_own = dot_t(q, kv[0, :, cols]) * SCALE2
        s_text = dot_t(q, tk[:, cols]) * SCALE2 + bias
        high = jnp.max(jnp.maximum(s_own, s_text), axis=1, keepdims=True)
        high = high.astype(BF).astype(F32)
        p_own = jnp.exp2(s_own - high)
        p_text = jnp.exp2(s_text - high)
        total = jnp.sum(p_own + p_text, axis=1, keepdims=True)
        acc = dot(p_own.astype(BF), kv[1, :, cols]) + dot(p_text.astype(BF), tv[:, cols])
        rows = slice(head * TEXT, (head + 1) * TEXT)
        acc_s[rows, :] = acc.astype(BF)
        high_s[rows, :] = jnp.broadcast_to(high, (TEXT, HEAD_DIM))
        total_s[rows, :] = jnp.broadcast_to(total, (TEXT, HEAD_DIM))

    for rank in range(PLANE):
        rows = slice(rank * EACH, (rank + 1) * EACH)
        out[rank, :EACH] = acc_s[rows, :]
        out[rank, EACH:] = stat_rows((high_s[rows, :], *split(total_s[rows, :])))


WHOLE = pl.BlockSpec(memory_space=pltpu.VMEM)
SCALARS = pl.BlockSpec(memory_space=pltpu.SMEM)
FAR = pl.BlockSpec(memory_space=pltpu.HBM)
ANY = pl.BlockSpec(memory_space=pl.ANY)


def text_part(pos, valid, tq, kv, tk, tv):
    count = HEADS_HERE * TEXT
    return pl.pallas_call(
        text_part_kernel,
        in_specs=[SCALARS, WHOLE, FAR, FAR, FAR, FAR],
        out_specs=WHOLE,
        out_shape=jax.ShapeDtypeStruct((PLANE, SLOT, HEAD_DIM), BF),
        scratch_shapes=[pltpu.VMEM(x.shape, BF) for x in (tq, kv, tk, tv)]
        + [pltpu.VMEM((count, HEAD_DIM), t) for t in (BF, F32, F32)]
        + [pltpu.SemaphoreType.DMA((2, 4))],
        cost_estimate=pl.CostEstimate(
            flops=5 * 10**9, bytes_accessed=2 << 20, transcendentals=10**6
        ),
        compiler_params=pltpu.CompilerParams(vmem_limit_bytes=VMEM),
        name="text_part",
    )(pos, valid, tq, kv, tk, tv)


def corners_kernel(own, z_low, z_high, after, low, high, held, sems):
    inward, outward = [], []
    for j, ref in enumerate((z_low, own, z_high)):
        for side, out in enumerate((low, high)):
            part = ref.at[:, pl.ds((1 - side) * PAIR, PAIR), :]
            inward.append(pltpu.make_async_copy(part, held.at[j, side], sems.at[0, j, side]))
            outward.append(pltpu.make_async_copy(held.at[j, side], out.at[j], sems.at[1, j, side]))
    for copy in inward:
        copy.start()
    for copy, onward in zip(inward, outward):
        copy.wait()
        onward.start()
    wait_all(outward)


def corners(own, z_low, z_high, after):
    shape = jax.ShapeDtypeStruct((3, 2, PAIR, WIDTH), BF)
    return pl.pallas_call(
        corners_kernel,
        in_specs=[ANY] * 4,
        out_specs=(ANY, ANY),
        out_shape=(shape, shape),
        scratch_shapes=[
            pltpu.VMEM((3, 2, 2, PAIR, WIDTH), BF),
            pltpu.SemaphoreType.DMA((2, 3, 2)),
        ],
        cost_estimate=pl.CostEstimate(flops=0, bytes_accessed=5 << 20, transcendentals=0),
        compiler_params=pltpu.CompilerParams(vmem_limit_bytes=VMEM),
        name="corners",
    )(own, z_low, z_high, after)


def merge_kernel(parts, w_h, z_low, z_high, out, w_out, w, sems):
    inward = pltpu.make_async_copy(w_h, w, sems.at[0])
    onward = pltpu.make_async_copy(w, w_out, sems.at[1])
    inward.start()
    combine_kernel(parts, out, between=lambda: (inward.wait(), onward.start()))
    onward.wait()


def combine_kernel(parts, out, between=lambda: None):
    sources, copies = parts.shape[0], out.shape[0]
    stats = [parts[i, EACH:].astype(F32) for i in range(sources)]
    highs = [s[0:1] for s in stats]
    high = functools.reduce(jnp.maximum, highs)
    weights = [jnp.exp2(h - high) for h in highs]
    total = sum(w * (s[1:2] + s[2:3]) for w, s in zip(weights, stats))
    finish = out.shape[1] == EACH
    if finish:
        lane = lax.broadcasted_iota(jnp.int32, (1, HEAD_DIM), 1)
        total = jnp.where(lane < EACH, total, 1.0)
        weights = [w / total for w in weights]
    row = lax.broadcasted_iota(jnp.int32, (HEAD_DIM, HEAD_DIM), 0)
    table = jnp.zeros((HEAD_DIM, HEAD_DIM), F32)
    for i, w in enumerate(weights):
        table = jnp.where(row == i, w, table)
    table = table.T
    between()
    sums = jnp.zeros((EACH, HEAD_DIM), F32)
    for i in range(sources):
        sums += table[:EACH, i : i + 1] * parts[i, :EACH].astype(F32)
    sums = sums.astype(BF)
    for at in range(copies):
        out[at, :EACH] = sums
    if not finish:
        lines = lay_out((high, *split(total)))
        for at in range(copies):
            out[at, EACH:] = lines


def merge(parts, copies, w, *after):
    return pl.pallas_call(
        merge_kernel,
        in_specs=[WHOLE, FAR] + [ANY] * len(after),
        out_specs=(WHOLE, FAR),
        out_shape=(
            jax.ShapeDtypeStruct((copies, SLOT, HEAD_DIM), BF),
            jax.ShapeDtypeStruct(w.shape, BF),
        ),
        scratch_shapes=[pltpu.VMEM(w.shape, BF), pltpu.SemaphoreType.DMA((2,))],
        cost_estimate=pl.CostEstimate(
            flops=10**9, bytes_accessed=2 << 20, transcendentals=0
        ),
        compiler_params=pltpu.CompilerParams(vmem_limit_bytes=16 << 20),
        name="text_merge",
    )(parts, w, *after)


def relay_kernel(low, high, after, low_out, high_out, held, sems):
    pairs = ((low, low_out), (high, high_out))
    inward = [
        pltpu.make_async_copy(ref, held.at[i], sems.at[0, i]) for i, (ref, _) in enumerate(pairs)
    ]
    onward = [
        pltpu.make_async_copy(held.at[i], out, sems.at[1, i]) for i, (_, out) in enumerate(pairs)
    ]
    for copy in inward:
        copy.start()
    for copy, following in zip(inward, onward):
        copy.wait()
        following.start()
    wait_all(onward)


def relay(low, high, after):
    return pl.pallas_call(
        relay_kernel,
        in_specs=[ANY] * 3,
        out_specs=(ANY, ANY),
        out_shape=[jax.ShapeDtypeStruct(x.shape, BF) for x in (low, high)],
        scratch_shapes=[pltpu.VMEM((2, *low.shape), BF), pltpu.SemaphoreType.DMA((2, 2))],
        cost_estimate=pl.CostEstimate(flops=0, bytes_accessed=4 << 20, transcendentals=0),
        compiler_params=pltpu.CompilerParams(vmem_limit_bytes=16 << 20),
        name="relay",
    )(low, high, after)


def finish_sums(parts, copies, *after):
    return pl.pallas_call(
        lambda parts, *rest: combine_kernel(parts, rest[-1]),
        in_specs=[WHOLE] + [ANY] * len(after),
        out_specs=WHOLE,
        out_shape=jax.ShapeDtypeStruct((copies, EACH, HEAD_DIM), BF),
        cost_estimate=pl.CostEstimate(
            flops=10**9, bytes_accessed=1 << 20, transcendentals=0
        ),
        compiler_params=pltpu.CompilerParams(vmem_limit_bytes=16 << 20),
        name="text_finish_sums",
    )(parts, *after)


def video_kernel(pos, mask, valid, *rest):
    far, out, near, bias_s, sems = rest[:8], rest[9], rest[10:18], rest[18], rest[19]
    q, tk, tv, own, z_low, z_high, t_low, t_high = near
    pairs = list(zip(far, near))
    begun = fetch(pairs, sems.at[0], FIRST)
    later = fetch(pairs, sems.at[1], REST)
    fill_bias(pos, mask, bias_s)
    text_bias = jnp.where(valid[...] > 0, 0.0, LOW)
    for head in range(HEADS_HERE):
        if head == 0:
            wait_all(begun)
        elif head == 1:
            wait_all(later)
        cols = slice(head * HEAD_DIM, (head + 1) * HEAD_DIM)
        one_head(
            q.at[:, cols],
            tk.at[:, cols],
            tv.at[:, cols],
            [ref.at[:, :, cols] for ref in (z_low, own, z_high)],
            [ref.at[:, :, :, cols] for ref in (t_low, t_high)],
            text_bias,
            bias_s,
            out.at[:, cols],
        )


def fill_bias(pos, mask, bias_s):
    row = lax.broadcasted_iota(jnp.int32, (8, PAIR), 0)
    col = lax.broadcasted_iota(jnp.int32, (8, PAIR), 1)
    second_q = row >= TILE
    second_k = jnp.bitwise_and(col, 7) >= TILE
    for a in range(2):
        for i in range(3):
            for j in range(3):
                where_t = pos[0] * 2 + a + i - 1
                where_h = pos[1] + j - 1
                inside = (where_t >= 0) & (where_t < pos[3]) & (where_h >= 0) & (where_h < pos[4])
                base = 9 * i + 3 * j

                def one(c, k):
                    if base + k == 13:
                        return jnp.where(inside, 0.0, LOW)
                    ok = inside & (mask[(a * 2 + c) * 27 + base + k] > 0)
                    return jnp.where(ok, 0.0, LOW)

                low = jnp.where(second_k, one(0, 2), one(0, 1))
                high = jnp.where(second_k, one(1, 1), one(1, 0))
                bias_s[a, i, j] = jnp.where(second_q, high, low)


def one_head(q, tk, tv, mids, sides, text_bias, bias_s, out):
    def rows(part):
        return (
            jnp.concatenate([sides[0][j, part] for j in range(3)], axis=0),
            jnp.concatenate(
                [ref[part, a * PAIR : (a + 1) * PAIR, :] for a in range(2) for ref in mids],
                axis=0,
            ),
            jnp.concatenate([sides[1][j, part] for j in range(3)], axis=0),
        )

    queries = q[...]
    k_low, k_mid, k_high = rows(0)
    v_low, v_mid, v_high = rows(1)
    s_mid = dot_t(queries, k_mid)
    s_text = dot_t(queries, tk[...])
    s_sides = (dot_t(queries[:PAIR], k_low), dot_t(queries[PAIR:], k_high))
    v_sides = (v_low, v_high)
    for a in range(2):
        mine = slice(a * PAIR, (a + 1) * PAIR)
        pieces = []
        for i in range(3):
            for j in range(3):
                at = (a + i - 1) * 3 + j
                if 0 <= a + i - 1 <= 1:
                    piece = s_mid[mine, at * PAIR : (at + 1) * PAIR]
                else:
                    piece = s_sides[a][:, j * PAIR : (j + 1) * PAIR]
                piece = piece.reshape(PAIR // 8, 8, PAIR) * SCALE2 + bias_s[a, i, j][None]
                pieces.append(piece.reshape(PAIR, PAIR))
        text_piece = s_text[mine] * SCALE2 + text_bias
        pieces.append(text_piece[:, :PAIR])
        pieces.append(text_piece[:, PAIR:])
        high = functools.reduce(jnp.maximum, pieces)
        high = jnp.max(high, axis=1, keepdims=True)
        weights = [jnp.exp2(piece - high) for piece in pieces]
        total = jnp.sum(functools.reduce(jnp.add, weights), axis=1, keepdims=True)
        weights = [w.astype(BF) for w in weights]
        side = weights[:3] if a == 0 else weights[6:9]
        mid = weights[3:9] if a == 0 else weights[:6]
        mixed = (
            dot(jnp.concatenate(side, axis=1), v_sides[a])
            + dot(jnp.concatenate(mid, axis=1), v_mid)
            + dot(jnp.concatenate(weights[9:], axis=1), tv[...])
        )
        out[mine, :] = (mixed / total).astype(BF)


def video_attention(pos, mask, valid, *arrays):
    return pl.pallas_call(
        video_kernel,
        in_specs=[SCALARS, SCALARS, WHOLE] + [FAR] * 4 + [ANY] * (len(arrays) - 4),
        out_specs=WHOLE,
        out_shape=jax.ShapeDtypeStruct((OWN, WIDTH), BF),
        scratch_shapes=[pltpu.VMEM(x.shape, BF) for x in arrays[:8]]
        + [pltpu.VMEM((2, 3, 3, 8, PAIR), F32), pltpu.SemaphoreType.DMA((2, 8))],
        cost_estimate=pl.CostEstimate(
            flops=9 * 10**9, bytes_accessed=6 << 20, transcendentals=2 * 10**6
        ),
        compiler_params=pltpu.CompilerParams(vmem_limit_bytes=VMEM),
        name="video_attention",
    )(pos, mask, valid, *arrays)


def project(pos, blocks, mine, held, sems, read, put, out, sent, out_sems):
    width = held.shape[1] // 4
    near, (top, bottom) = blocks[:7], blocks[7:]
    half = top.shape[0]
    for step, ref in list(zip((0, 1, 2, 3, 5, 6, 7), near)) + [(4, None)]:
        column = jnp.bitwise_and(pos[1] + step, 7)
        is_mine = lax.shift_right_logical(column, 2) == pos[2]
        slot = jnp.bitwise_and(column, 3)
        columns = pl.ds(pl.multiple_of(slot * width, width), width)

        @pl.when(is_mine if mine else jnp.logical_not(is_mine))
        def _():
            if ref is None:
                for part, piece in enumerate((top, bottom)):
                    target = held.at[part * half : (part + 1) * half, columns]
                    pltpu.make_async_copy(piece, target, sems.at[slot]).start()
            else:
                pltpu.make_async_copy(ref, held.at[:, columns], sems.at[slot]).start()

    left = read()
    copies = []
    for pair in range(2):
        for slot in (2 * pair, 2 * pair + 1):
            columns = slice(slot * width, (slot + 1) * width)
            pltpu.make_async_copy(near[0], held.at[:, columns], sems.at[slot]).wait()
        columns = slice(2 * pair * width, 2 * (pair + 1) * width)
        sent[:, columns] = put(columns, dot(left, held[:, columns])).astype(BF)
        copies.append(
            pltpu.make_async_copy(sent.at[:, columns], out.at[:, columns], out_sems.at[pair])
        )
        copies[-1].start()
    wait_all(copies)


def text_share_kernel(pos, parts_h, *rest):
    blocks, rest = rest[:9], rest[9:]
    rows, share, parts, in_sems, held, sent, sems, out_sems = rest
    copy = pltpu.make_async_copy(parts_h, parts, in_sems.at[0])
    copy.start()

    def read():
        copy.wait()
        flat = parts[...].reshape(HEADS_HERE * TEXT, HEAD_DIM)
        heads = [flat[head * TEXT : (head + 1) * TEXT] for head in range(HEADS_HERE)]
        rows[...] = jnp.concatenate(heads, axis=1)
        return rows[...]

    project(pos, blocks, False, held, sems, read, lambda _, x: x, share, sent, out_sems)


def share_kernel(pos, rows_h, *rest):
    blocks, rest = rest[:9], rest[9:]
    share, rows, in_sems, held, sent, sems, out_sems = rest
    copy = pltpu.make_async_copy(rows_h, rows, in_sems.at[0])
    copy.start()

    def read():
        copy.wait()
        return rows[...]

    project(pos, blocks, False, held, sems, read, lambda _, x: x, share, sent, out_sems)


def finish_kernel(pos, rows_h, other_h, *rest):
    blocks, rest = rest[:9], rest[9:]
    out, rows, other, in_sems, held, sent, sems, out_sems = rest
    copies = [
        pltpu.make_async_copy(rows_h, rows, in_sems.at[0]),
        pltpu.make_async_copy(other_h, other, in_sems.at[1]),
    ]
    for copy in copies:
        copy.start()

    def read():
        wait_all(copies)
        return rows[...]

    def put(columns, terms):
        return terms + other[:, columns].astype(F32)

    project(pos, blocks, True, held, sems, read, put, out, sent, out_sems)


def project_call(kernel, name, pos, left, blocks, out_shape, out_specs, scratch):
    depth, width = blocks[0].shape
    return pl.pallas_call(
        kernel,
        in_specs=[SCALARS] + [ANY] * len(left) + [FAR] * 7 + [ANY] * 2,
        out_specs=out_specs,
        out_shape=out_shape,
        scratch_shapes=[pltpu.VMEM(x.shape, BF) for x in left]
        + scratch
        + [
            pltpu.SemaphoreType.DMA((2,)),
            pltpu.VMEM((depth, 4 * width), BF),
            pltpu.VMEM((TEXT, 4 * width), BF),
            pltpu.SemaphoreType.DMA((4,)),
            pltpu.SemaphoreType.DMA((2,)),
        ],
        cost_estimate=pl.CostEstimate(
            flops=8 * TEXT * depth * width, bytes_accessed=4 << 20, transcendentals=0
        ),
        compiler_params=pltpu.CompilerParams(vmem_limit_bytes=24 << 20),
        name=name,
    )(pos, *left, *blocks)


def shards(video_q, video_kv, text_q, text_k, text_v, tile_mask, text_valid, w_out):
    frames, rows, cols, width = video_q.shape
    t_count, h_count = lax.axis_size("tm"), lax.axis_size("height")
    zero = jnp.int32(0)
    pos = jnp.stack(
        [
            lax.axis_index("tm"),
            lax.axis_index("height"),
            lax.axis_index("head"),
            zero + t_count * 2,
            zero + h_count,
        ]
    ).astype(jnp.int32)
    mask = tile_mask.reshape(-1)
    valid = text_valid.reshape(1, TEXT)
    own = video_kv.reshape(2, OWN, width)
    q = video_q.reshape(OWN, width)

    def up(x, axis):
        n = lax.axis_size(axis)
        return lax.ppermute(x, axis, [(i, (i + 1) % n) for i in range(n)])

    def down(x, axis):
        n = lax.axis_size(axis)
        return lax.ppermute(x, axis, [((i + 1) % n, i) for i in range(n)])

    z_low, z_high = up(own, "height"), down(own, "height")
    parts = text_part(pos, valid, text_q, own, text_k, text_v)
    parts = lax.all_to_all(parts, "tm", 0, 0, tiled=True)
    parts, ring = merge(parts, lax.axis_size("height"), w_out, z_low, z_high)
    low, high = corners(own, z_low, z_high, parts)
    t_low, t_high = up(low, "tm"), down(high, "tm")

    parts = lax.all_to_all(parts, "height", 0, 0, tiled=True)
    before, after = [], []
    for step in range(3):
        low, high = (before[-1], after[-1]) if step else (ring, ring)
        if step == 2:
            low, high = relay(low, high, parts)
        before.append(up(low, "height"))
        after.append(down(high, "height"))
    half = w_out.shape[0] // 2
    far = [up(before[2][:half], "height"), down(after[2][half:], "height")]

    sums = finish_sums(parts, lax.axis_size("tm"), t_low, t_high)
    parts = lax.all_to_all(sums, "tm", 0, 0, tiled=True)

    video_rows = video_attention(
        pos, mask, valid, q, text_k, text_v, own, z_low, z_high, t_low, t_high, sums
    )

    def swap(x):
        return lax.ppermute(x, "head", [(0, 1), (1, 0)])

    blocks = [w_out] + after + before[::-1] + far
    full = jax.ShapeDtypeStruct((OWN, 4 * w_out.shape[1]), BF)
    video_other = swap(
        project_call(share_kernel, "video_share", pos, [video_rows], blocks, full, FAR, [])
    )
    text_rows, text_other = project_call(
        text_share_kernel,
        "text_share",
        pos,
        [parts],
        blocks,
        (jax.ShapeDtypeStruct((TEXT, WIDTH), BF), full),
        (WHOLE, FAR),
        [],
    )
    text_other = swap(text_other)
    video_out = project_call(
        finish_kernel, "video_finish", pos, [video_rows, video_other], blocks, full, FAR, []
    )
    text_out = project_call(
        finish_kernel, "text_finish", pos, [text_rows, text_other], blocks, full, FAR, []
    )
    return video_out.reshape(frames, rows, cols, -1), text_out


def solution(mesh):
    return jax.shard_map(
        shards,
        mesh=mesh,
        in_specs=(
            P("tm", "height", None, "head"),
            P(None, "tm", "height", None, "head"),
            P(None, "head"),
            P(None, "head"),
            P(None, "head"),
            P("tm", "height", None, None),
            P(),
            P("head", "height"),
        ),
        out_specs=(P("tm", "height", None, "head"), P(None, "head")),
        check_vma=False,
    )
```

```python
import functools

import jax
import jax.numpy as jnp
from jax import lax
from jax.experimental import pallas as pl
from jax.experimental.pallas import tpu as pltpu
from jax.sharding import PartitionSpec as P

HEAD_DIM = 128
TILE = 4
HEADS_HERE = 6
PAIR = 128
OWN = 256
TEXT = 256
WIDTH = HEADS_HERE * HEAD_DIM
PLANE = 16
EACH = HEADS_HERE * TEXT // PLANE
SLOT = 112
SCALE2 = HEAD_DIM ** (-0.5) * 1.4426950408889634
LOW = -1e30
VMEM = 60 << 20
BF = jnp.bfloat16
F32 = jnp.float32


def dot_t(a, b):
    return lax.dot_general(a, b, (((1,), (1,)), ((), ())), preferred_element_type=F32)


def dot(a, b):
    return jnp.dot(a, b, preferred_element_type=F32)


def fetch(pairs, sems, columns):
    copies = []
    for at, (source, target) in enumerate(pairs):
        where = (slice(None),) * (len(source.shape) - 1) + (columns,)
        copies.append(pltpu.make_async_copy(source.at[where], target.at[where], sems.at[at]))
    for copy in copies:
        copy.start()
    return copies


def wait_all(copies):
    for copy in copies:
        copy.wait()


FIRST, REST = slice(0, HEAD_DIM), slice(HEAD_DIM, WIDTH)


def stat_rows(values):
    row = lax.broadcasted_iota(jnp.int32, (EACH, HEAD_DIM), 0)
    col = lax.broadcasted_iota(jnp.int32, (EACH, HEAD_DIM), 1)
    lines = [jnp.sum(jnp.where(row == col, v, 0.0), axis=0, keepdims=True) for v in values]
    return lay_out(lines)


def lay_out(lines):
    row = lax.broadcasted_iota(jnp.int32, (SLOT - EACH, HEAD_DIM), 0)
    full = jnp.zeros((SLOT - EACH, HEAD_DIM), F32)
    for at, line in enumerate(lines):
        full = jnp.where(row == at, line, full)
    return full.astype(BF)


def split(total):
    high = total.astype(BF).astype(F32)
    return high, total - high


def text_part_kernel(
    pos, valid, tq_h, kv_h, tk_h, tv_h, w_h, out, w_out, tq, kv, tk, tv, w, acc_s, high_s, total_s, sems, w_sems
):
    inward = pltpu.make_async_copy(w_h, w, w_sems.at[0])
    onward = pltpu.make_async_copy(w, w_out, w_sems.at[1])
    pairs = [(tq_h, tq), (kv_h, kv), (tk_h, tk), (tv_h, tv)]
    begun = fetch(pairs, sems.at[0], FIRST)
    later = fetch(pairs, sems.at[1], REST)
    inward.start()
    first = (pos[0] == 0) & (pos[1] == 0)
    bias = jnp.where((valid[...] > 0) & first, 0.0, LOW)
    for head in range(HEADS_HERE):
        if head == 0:
            wait_all(begun)
        elif head == 1:
            wait_all(later)
            inward.wait()
            onward.start()
        cols = slice(head * HEAD_DIM, (head + 1) * HEAD_DIM)
        q = tq[:, cols]
        s_own = dot_t(q, kv[0, :, cols]) * SCALE2
        s_text = dot_t(q, tk[:, cols]) * SCALE2 + bias
        high = jnp.max(jnp.maximum(s_own, s_text), axis=1, keepdims=True)
        high = high.astype(BF).astype(F32)
        p_own = jnp.exp2(s_own - high)
        p_text = jnp.exp2(s_text - high)
        total = jnp.sum(p_own + p_text, axis=1, keepdims=True)
        acc = dot(p_own.astype(BF), kv[1, :, cols]) + dot(p_text.astype(BF), tv[:, cols])
        rows = slice(head * TEXT, (head + 1) * TEXT)
        acc_s[rows, :] = acc.astype(BF)
        high_s[rows, :] = jnp.broadcast_to(high, (TEXT, HEAD_DIM))
        total_s[rows, :] = jnp.broadcast_to(total, (TEXT, HEAD_DIM))

    for rank in range(PLANE):
        rows = slice(rank * EACH, (rank + 1) * EACH)
        out[rank, :EACH] = acc_s[rows, :]
        out[rank, EACH:] = stat_rows((high_s[rows, :], *split(total_s[rows, :])))
    onward.wait()


WHOLE = pl.BlockSpec(memory_space=pltpu.VMEM)
SCALARS = pl.BlockSpec(memory_space=pltpu.SMEM)
FAR = pl.BlockSpec(memory_space=pltpu.HBM)
ANY = pl.BlockSpec(memory_space=pl.ANY)


def text_part(pos, valid, tq, kv, tk, tv, w):
    count = HEADS_HERE * TEXT
    return pl.pallas_call(
        text_part_kernel,
        in_specs=[SCALARS, WHOLE, FAR, FAR, FAR, FAR, FAR],
        out_specs=(WHOLE, FAR),
        out_shape=(
            jax.ShapeDtypeStruct((PLANE, SLOT, HEAD_DIM), BF),
            jax.ShapeDtypeStruct(w.shape, BF),
        ),
        scratch_shapes=[pltpu.VMEM(x.shape, BF) for x in (tq, kv, tk, tv, w)]
        + [pltpu.VMEM((count, HEAD_DIM), t) for t in (BF, F32, F32)]
        + [pltpu.SemaphoreType.DMA((2, 4)), pltpu.SemaphoreType.DMA((2,))],
        cost_estimate=pl.CostEstimate(
            flops=5 * 10**9, bytes_accessed=2 << 20, transcendentals=10**6
        ),
        compiler_params=pltpu.CompilerParams(vmem_limit_bytes=VMEM),
        name="text_part",
    )(pos, valid, tq, kv, tk, tv, w)


def merge_kernel(parts, own, z_low, z_high, out, low, high, held, sems):
    inward, outward = [], []
    for j, ref in enumerate((z_low, own, z_high)):
        for side, target in enumerate((low, high)):
            part = ref.at[:, pl.ds((1 - side) * PAIR, PAIR), :]
            inward.append(pltpu.make_async_copy(part, held.at[j, side], sems.at[0, j, side]))
            outward.append(
                pltpu.make_async_copy(held.at[j, side], target.at[j], sems.at[1, j, side])
            )
    for copy in inward:
        copy.start()

    def between():
        for copy, onward in zip(inward, outward):
            copy.wait()
            onward.start()

    combine_kernel(1, parts, out, between=between)
    wait_all(outward)


def merge(parts, copies, own, z_low, z_high):
    shape = jax.ShapeDtypeStruct((3, 2, PAIR, WIDTH), BF)
    return pl.pallas_call(
        merge_kernel,
        in_specs=[WHOLE] + [ANY] * 3,
        out_specs=(WHOLE, ANY, ANY),
        out_shape=(jax.ShapeDtypeStruct((copies, SLOT, HEAD_DIM), BF), shape, shape),
        scratch_shapes=[
            pltpu.VMEM((3, 2, 2, PAIR, WIDTH), BF),
            pltpu.SemaphoreType.DMA((2, 3, 2)),
        ],
        cost_estimate=pl.CostEstimate(
            flops=2 * 10**9, bytes_accessed=6 << 20, transcendentals=0
        ),
        compiler_params=pltpu.CompilerParams(vmem_limit_bytes=24 << 20),
        name="text_merge",
    )(parts, own, z_low, z_high)


def combine_kernel(count, *refs, between=lambda: None):
    ins, out = refs[:count], refs[-1]
    parts = [ref.at[i] for ref in ins for i in range(ref.shape[0])]
    stats = [part[EACH:].astype(F32) for part in parts]
    highs = [s[0:1] for s in stats]
    high = functools.reduce(jnp.maximum, highs)
    weights = [jnp.exp2(h - high) for h in highs]
    total = sum(w * (s[1:2] + s[2:3]) for w, s in zip(weights, stats))
    finish = out.shape[1] == EACH
    if finish:
        lane = lax.broadcasted_iota(jnp.int32, (1, HEAD_DIM), 1)
        total = jnp.where(lane < EACH, total, 1.0)
        weights = [w / total for w in weights]
    row = lax.broadcasted_iota(jnp.int32, (HEAD_DIM, HEAD_DIM), 0)
    table = jnp.zeros((HEAD_DIM, HEAD_DIM), F32)
    for i, w in enumerate(weights):
        table = jnp.where(row == i, w, table)
    table = table.T
    between()
    sums = jnp.zeros((EACH, HEAD_DIM), F32)
    for i, part in enumerate(parts):
        sums += table[:EACH, i : i + 1] * part[:EACH].astype(F32)
    sums = sums.astype(BF)
    for at in range(out.shape[0]):
        out[at, :EACH] = sums
    if not finish:
        lines = lay_out((high, *split(total)))
        for at in range(out.shape[0]):
            out[at, EACH:] = lines


def combine(parts, copies, finish, name, *after):
    return pl.pallas_call(
        functools.partial(combine_kernel, len(parts)),
        in_specs=[WHOLE] * len(parts) + [ANY] * len(after),
        out_specs=WHOLE,
        out_shape=jax.ShapeDtypeStruct((copies, EACH if finish else SLOT, HEAD_DIM), BF),
        cost_estimate=pl.CostEstimate(
            flops=10**9, bytes_accessed=1 << 20, transcendentals=0
        ),
        compiler_params=pltpu.CompilerParams(vmem_limit_bytes=16 << 20),
        name=name,
    )(*parts, *after)


def relay_kernel(low, high, *rest):
    low_out, high_out, held, sems = rest[-4:]
    pairs = ((low, low_out), (high, high_out))
    inward = [
        pltpu.make_async_copy(ref, held.at[i], sems.at[0, i]) for i, (ref, _) in enumerate(pairs)
    ]
    onward = [
        pltpu.make_async_copy(held.at[i], out, sems.at[1, i]) for i, (_, out) in enumerate(pairs)
    ]
    for copy in inward:
        copy.start()
    for copy, following in zip(inward, onward):
        copy.wait()
        following.start()
    wait_all(onward)


def halves_kernel(low, high, after, low_out, high_out, held, sems):
    half = low_out.shape[0]
    inward = [
        pltpu.make_async_copy(ref, held.at[i], sems.at[0, i])
        for i, ref in enumerate((low.at[0:half], high.at[half : 2 * half]))
    ]
    onward = [
        pltpu.make_async_copy(held.at[i], out, sems.at[1, i])
        for i, out in enumerate((low_out, high_out))
    ]
    for copy in inward:
        copy.start()
    for copy, following in zip(inward, onward):
        copy.wait()
        following.start()
    wait_all(onward)


def halves(low, high, after):
    shape = (low.shape[0] // 2, low.shape[1])
    return pl.pallas_call(
        halves_kernel,
        in_specs=[ANY] * 3,
        out_specs=(ANY, ANY),
        out_shape=[jax.ShapeDtypeStruct(shape, BF)] * 2,
        scratch_shapes=[pltpu.VMEM((2, *shape), BF), pltpu.SemaphoreType.DMA((2, 2))],
        cost_estimate=pl.CostEstimate(flops=0, bytes_accessed=2 << 20, transcendentals=0),
        compiler_params=pltpu.CompilerParams(vmem_limit_bytes=16 << 20),
        name="halves",
    )(low, high, after)


def relay(low, high, *after):
    return pl.pallas_call(
        relay_kernel,
        in_specs=[ANY] * (2 + len(after)),
        out_specs=(ANY, ANY),
        out_shape=[jax.ShapeDtypeStruct(x.shape, BF) for x in (low, high)],
        scratch_shapes=[pltpu.VMEM((2, *low.shape), BF), pltpu.SemaphoreType.DMA((2, 2))],
        cost_estimate=pl.CostEstimate(flops=0, bytes_accessed=4 << 20, transcendentals=0),
        compiler_params=pltpu.CompilerParams(vmem_limit_bytes=16 << 20),
        name="relay",
    )(low, high, *after)


def video_kernel(pos, mask, valid, *rest):
    far, out_h, near, out, bias_s, sems = rest[:8], rest[8], rest[9:17], *rest[17:]
    q, tk, tv, own, z_low, z_high, t_low, t_high = near
    pairs = list(zip(far, near))
    begun = fetch(pairs, sems.at[0], FIRST)
    later = fetch(pairs, sems.at[1], REST)
    fill_bias(pos, mask, bias_s)
    text_bias = jnp.where(valid[...] > 0, 0.0, LOW)
    for head in range(HEADS_HERE):
        if head == 0:
            wait_all(begun)
        elif head == 1:
            wait_all(later)
        cols = slice(head * HEAD_DIM, (head + 1) * HEAD_DIM)
        one_head(
            q.at[:, cols],
            tk.at[:, cols],
            tv.at[:, cols],
            [ref.at[:, :, cols] for ref in (z_low, own, z_high)],
            [ref.at[:, :, :, cols] for ref in (t_low, t_high)],
            text_bias,
            bias_s,
            out.at[:, cols],
        )
    copy = pltpu.make_async_copy(out, out_h, sems.at[0, 0])
    copy.start()
    copy.wait()


def fill_bias(pos, mask, bias_s):
    row = lax.broadcasted_iota(jnp.int32, (8, PAIR), 0)
    col = lax.broadcasted_iota(jnp.int32, (8, PAIR), 1)
    second_q = row >= TILE
    second_k = jnp.bitwise_and(col, 7) >= TILE
    for a in range(2):
        for i in range(3):
            for j in range(3):
                where_t = pos[0] * 2 + a + i - 1
                where_h = pos[1] + j - 1
                inside = (where_t >= 0) & (where_t < pos[3]) & (where_h >= 0) & (where_h < pos[4])
                base = 9 * i + 3 * j

                def one(c, k):
                    if base + k == 13:
                        return jnp.where(inside, 0.0, LOW)
                    ok = inside & (mask[(a * 2 + c) * 27 + base + k] > 0)
                    return jnp.where(ok, 0.0, LOW)

                low = jnp.where(second_k, one(0, 2), one(0, 1))
                high = jnp.where(second_k, one(1, 1), one(1, 0))
                bias_s[a, i, j] = jnp.where(second_q, high, low)


def one_head(q, tk, tv, mids, sides, text_bias, bias_s, out):
    def rows(part):
        return (
            jnp.concatenate([sides[0][j, part] for j in range(3)], axis=0),
            jnp.concatenate(
                [ref[part, a * PAIR : (a + 1) * PAIR, :] for a in range(2) for ref in mids],
                axis=0,
            ),
            jnp.concatenate([sides[1][j, part] for j in range(3)], axis=0),
        )

    queries = q[...]
    k_low, k_mid, k_high = rows(0)
    v_low, v_mid, v_high = rows(1)
    s_mid = dot_t(queries, k_mid)
    s_text = dot_t(queries, tk[...])
    s_sides = (dot_t(queries[:PAIR], k_low), dot_t(queries[PAIR:], k_high))
    v_sides = (v_low, v_high)
    for a in range(2):
        mine = slice(a * PAIR, (a + 1) * PAIR)
        pieces = []
        for i in range(3):
            for j in range(3):
                at = (a + i - 1) * 3 + j
                if 0 <= a + i - 1 <= 1:
                    piece = s_mid[mine, at * PAIR : (at + 1) * PAIR]
                else:
                    piece = s_sides[a][:, j * PAIR : (j + 1) * PAIR]
                piece = piece.reshape(PAIR // 8, 8, PAIR) * SCALE2 + bias_s[a, i, j][None]
                pieces.append(piece.reshape(PAIR, PAIR))
        text_piece = s_text[mine] * SCALE2 + text_bias
        pieces.append(text_piece[:, :PAIR])
        pieces.append(text_piece[:, PAIR:])
        high = functools.reduce(jnp.maximum, pieces)
        high = jnp.max(high, axis=1, keepdims=True)
        weights = [jnp.exp2(piece - high) for piece in pieces]
        total = jnp.sum(functools.reduce(jnp.add, weights), axis=1, keepdims=True)
        weights = [w.astype(BF) for w in weights]
        side = weights[:3] if a == 0 else weights[6:9]
        mid = weights[3:9] if a == 0 else weights[:6]
        mixed = (
            dot(jnp.concatenate(side, axis=1), v_sides[a])
            + dot(jnp.concatenate(mid, axis=1), v_mid)
            + dot(jnp.concatenate(weights[9:], axis=1), tv[...])
        )
        out[mine, :] = (mixed / total).astype(BF)


def video_attention(pos, mask, valid, *arrays):
    return pl.pallas_call(
        video_kernel,
        in_specs=[SCALARS, SCALARS, WHOLE] + [FAR] * 4 + [ANY] * (len(arrays) - 4),
        out_specs=FAR,
        out_shape=jax.ShapeDtypeStruct((OWN, WIDTH), BF),
        scratch_shapes=[pltpu.VMEM(x.shape, BF) for x in arrays[:8]]
        + [pltpu.VMEM((OWN, WIDTH), BF), pltpu.VMEM((2, 3, 3, 8, PAIR), F32), pltpu.SemaphoreType.DMA((2, 8))],
        cost_estimate=pl.CostEstimate(
            flops=9 * 10**9, bytes_accessed=6 << 20, transcendentals=2 * 10**6
        ),
        compiler_params=pltpu.CompilerParams(vmem_limit_bytes=VMEM),
        name="video_attention",
    )(pos, mask, valid, *arrays)


def project(pos, blocks, mine, held, sems, read, put, out, sent, out_sems):
    width = held.shape[1] // 4
    near, (top, bottom) = blocks[:7], blocks[7:]
    half = top.shape[0]
    for step, ref in list(zip((0, 1, 2, 3, 5, 6, 7), near)) + [(4, None)]:
        column = jnp.bitwise_and(pos[1] + step, 7)
        is_mine = lax.shift_right_logical(column, 2) == pos[2]
        slot = jnp.bitwise_and(column, 3)
        columns = pl.ds(pl.multiple_of(slot * width, width), width)

        @pl.when(is_mine if mine else jnp.logical_not(is_mine))
        def _():
            if ref is None:
                for part, piece in enumerate((top, bottom)):
                    target = held.at[part * half : (part + 1) * half, columns]
                    pltpu.make_async_copy(piece, target, sems.at[slot]).start()
            else:
                pltpu.make_async_copy(ref, held.at[:, columns], sems.at[slot]).start()

    left = read()
    copies = []
    for pair in range(2):
        for slot in (2 * pair, 2 * pair + 1):
            columns = slice(slot * width, (slot + 1) * width)
            pltpu.make_async_copy(near[0], held.at[:, columns], sems.at[slot]).wait()
        columns = slice(2 * pair * width, 2 * (pair + 1) * width)
        sent[:, columns] = put(columns, dot(left, held[:, columns])).astype(BF)
        copies.append(
            pltpu.make_async_copy(sent.at[:, columns], out.at[:, columns], out_sems.at[pair])
        )
        copies[-1].start()
    wait_all(copies)


def text_share_kernel(pos, parts_h, *rest):
    blocks, rest = rest[:9], rest[9:]
    rows_h, share, parts, rows, in_sems, held, sent, sems, out_sems = rest
    rows_copy = pltpu.make_async_copy(rows, rows_h, in_sems.at[1])
    copy = pltpu.make_async_copy(parts_h, parts, in_sems.at[0])
    copy.start()

    def read():
        copy.wait()
        flat = parts[...].reshape(HEADS_HERE * TEXT, HEAD_DIM)
        heads = [flat[head * TEXT : (head + 1) * TEXT] for head in range(HEADS_HERE)]
        rows[...] = jnp.concatenate(heads, axis=1)
        rows_copy.start()
        return rows[...]

    project(pos, blocks, False, held, sems, read, lambda _, x: x, share, sent, out_sems)
    rows_copy.wait()


def share_kernel(pos, rows_h, *rest):
    blocks, rest = rest[:9], rest[9:]
    share, rows, in_sems, held, sent, sems, out_sems = rest
    copy = pltpu.make_async_copy(rows_h, rows, in_sems.at[0])
    copy.start()

    def read():
        copy.wait()
        return rows[...]

    project(pos, blocks, False, held, sems, read, lambda _, x: x, share, sent, out_sems)


def finish_kernel(pos, rows_h, other_h, *rest):
    blocks, rest = rest[:9], rest[9:]
    out, rows, other, in_sems, held, sent, sems, out_sems = rest
    copies = [
        pltpu.make_async_copy(rows_h, rows, in_sems.at[0]),
        pltpu.make_async_copy(other_h, other, in_sems.at[1]),
    ]
    for copy in copies:
        copy.start()

    def read():
        wait_all(copies)
        return rows[...]

    def put(columns, terms):
        return terms + other[:, columns].astype(F32)

    project(pos, blocks, True, held, sems, read, put, out, sent, out_sems)


def project_call(kernel, name, pos, left, blocks, out_shape, out_specs, scratch):
    depth, width = blocks[0].shape
    return pl.pallas_call(
        kernel,
        in_specs=[SCALARS] + [FAR] + [ANY] * (len(left) - 1) + [FAR] * 7 + [ANY] * 2,
        out_specs=out_specs,
        out_shape=out_shape,
        scratch_shapes=[pltpu.VMEM(x.shape, BF) for x in left]
        + scratch
        + [
            pltpu.SemaphoreType.DMA((2,)),
            pltpu.VMEM((depth, 4 * width), BF),
            pltpu.VMEM((TEXT, 4 * width), BF),
            pltpu.SemaphoreType.DMA((4,)),
            pltpu.SemaphoreType.DMA((2,)),
        ],
        cost_estimate=pl.CostEstimate(
            flops=8 * TEXT * depth * width, bytes_accessed=4 << 20, transcendentals=0
        ),
        compiler_params=pltpu.CompilerParams(vmem_limit_bytes=24 << 20),
        name=name,
    )(pos, *left, *blocks)


def shards(video_q, video_kv, text_q, text_k, text_v, tile_mask, text_valid, w_out):
    frames, rows, cols, width = video_q.shape
    t_count, h_count = lax.axis_size("tm"), lax.axis_size("height")
    zero = jnp.int32(0)
    pos = jnp.stack(
        [
            lax.axis_index("tm"),
            lax.axis_index("height"),
            lax.axis_index("head"),
            zero + t_count * 2,
            zero + h_count,
        ]
    ).astype(jnp.int32)
    mask = tile_mask.reshape(-1)
    valid = text_valid.reshape(1, TEXT)
    own = video_kv.reshape(2, OWN, width)
    q = video_q.reshape(OWN, width)

    def up(x, axis, by=1):
        n = lax.axis_size(axis)
        return lax.ppermute(x, axis, [(i, (i + by) % n) for i in range(n)])

    def down(x, axis, by=1):
        return up(x, axis, -by)

    z_low, z_high = up(own, "height"), down(own, "height")
    parts, ring = text_part(pos, valid, text_q, own, text_k, text_v, w_out)
    before, after = [up(ring, "height")], [down(ring, "height")]
    parts = lax.all_to_all(parts, "tm", 0, 0, tiled=True)
    parts, low, high = merge(parts, h_count, own, z_low, z_high)
    t_low, t_high = up(low, "tm"), down(high, "tm")

    parts = lax.all_to_all(parts, "height", 0, 0, tiled=True)
    low, high = before[0], after[0]
    before.append(up(low, "height"))
    after.append(down(high, "height"))
    sums = combine([parts], t_count, True, "text_finish_sums")
    parts = lax.all_to_all(sums, "tm", 0, 0, tiled=True)
    low, high = relay(before[1], after[1], parts, t_low, t_high)
    before.append(up(low, "height"))
    after.append(down(high, "height"))
    video_rows = video_attention(
        pos, mask, valid, q, text_k, text_v, own, z_low, z_high, t_low, t_high
    )
    low, high = halves(before[2], after[2], video_rows)
    far = [up(low, "height"), down(high, "height")]

    def swap(x):
        return lax.ppermute(x, "head", [(0, 1), (1, 0)])

    blocks = [w_out] + after + before[::-1] + far
    full = jax.ShapeDtypeStruct((OWN, 4 * w_out.shape[1]), BF)
    video_other = swap(
        project_call(share_kernel, "video_share", pos, [video_rows], blocks, full, FAR, [])
    )
    text_rows, text_other = project_call(
        text_share_kernel,
        "text_share",
        pos,
        [parts],
        blocks,
        (jax.ShapeDtypeStruct((TEXT, WIDTH), BF), full),
        (FAR, FAR),
        [pltpu.VMEM((TEXT, WIDTH), BF)],
    )
    text_other = swap(text_other)
    video_out = project_call(
        finish_kernel, "video_finish", pos, [video_rows, video_other], blocks, full, FAR, []
    )
    text_out = project_call(
        finish_kernel, "text_finish", pos, [text_rows, text_other], blocks, full, FAR, []
    )
    return video_out.reshape(frames, rows, cols, -1), text_out


def solution(mesh):
    return jax.shard_map(
        shards,
        mesh=mesh,
        in_specs=(
            P("tm", "height", None, "head"),
            P(None, "tm", "height", None, "head"),
            P(None, "head"),
            P(None, "head"),
            P(None, "head"),
            P("tm", "height", None, None),
            P(),
            P("head", "height"),
        ),
        out_specs=(P("tm", "height", None, "head"), P(None, "head")),
        check_vma=False,
    )
```

```python
import functools

import jax
import jax.numpy as jnp
from jax import lax
from jax.experimental import pallas as pl
from jax.experimental.pallas import tpu as pltpu
from jax.sharding import PartitionSpec as P

HEAD_DIM = 128
TILE = 4
HEADS_HERE = 6
PAIR = 128
OWN = 256
TEXT = 256
WIDTH = HEADS_HERE * HEAD_DIM
PLANE = 16
EACH = HEADS_HERE * TEXT // PLANE
SLOT = 112
SCALE2 = HEAD_DIM ** (-0.5) * 1.4426950408889634
LOW = -1e30
VMEM = 60 << 20
BF = jnp.bfloat16
F32 = jnp.float32


def dot_t(a, b):
    return lax.dot_general(a, b, (((1,), (1,)), ((), ())), preferred_element_type=F32)


def dot(a, b):
    return jnp.dot(a, b, preferred_element_type=F32)


def fetch(pairs, sems, columns):
    copies = []
    for at, (source, target) in enumerate(pairs):
        where = (slice(None),) * (len(source.shape) - 1) + (columns,)
        copies.append(pltpu.make_async_copy(source.at[where], target.at[where], sems.at[at]))
    for copy in copies:
        copy.start()
    return copies


def wait_all(copies):
    for copy in copies:
        copy.wait()


FIRST, REST = slice(0, HEAD_DIM), slice(HEAD_DIM, WIDTH)


def stat_rows(values):
    row = lax.broadcasted_iota(jnp.int32, (EACH, HEAD_DIM), 0)
    col = lax.broadcasted_iota(jnp.int32, (EACH, HEAD_DIM), 1)
    lines = [jnp.sum(jnp.where(row == col, v, 0.0), axis=0, keepdims=True) for v in values]
    return lay_out(lines)


def lay_out(lines):
    row = lax.broadcasted_iota(jnp.int32, (SLOT - EACH, HEAD_DIM), 0)
    full = jnp.zeros((SLOT - EACH, HEAD_DIM), F32)
    for at, line in enumerate(lines):
        full = jnp.where(row == at, line, full)
    return full.astype(BF)


def split(total):
    high = total.astype(BF).astype(F32)
    return high, total - high


def text_part_kernel(
    pos, valid, tq_h, kv_h, tk_h, tv_h, w_h, out, w_out, tq, kv, tk, tv, w, acc_s, high_s, total_s, sems, w_sems
):
    inward = pltpu.make_async_copy(w_h, w, w_sems.at[0])
    onward = pltpu.make_async_copy(w, w_out, w_sems.at[1])
    pairs = [(tq_h, tq), (kv_h, kv), (tk_h, tk), (tv_h, tv)]
    begun = fetch(pairs, sems.at[0], FIRST)
    later = fetch(pairs, sems.at[1], REST)
    inward.start()
    first = (pos[0] == 0) & (pos[1] == 0)
    bias = jnp.where((valid[...] > 0) & first, 0.0, LOW)
    for head in range(HEADS_HERE):
        if head == 0:
            wait_all(begun)
        elif head == 1:
            wait_all(later)
            inward.wait()
            onward.start()
        cols = slice(head * HEAD_DIM, (head + 1) * HEAD_DIM)
        q = tq[:, cols]
        s_own = dot_t(q, kv[0, :, cols]) * SCALE2
        s_text = dot_t(q, tk[:, cols]) * SCALE2 + bias
        high = jnp.max(jnp.maximum(s_own, s_text), axis=1, keepdims=True)
        high = high.astype(BF).astype(F32)
        p_own = jnp.exp2(s_own - high)
        p_text = jnp.exp2(s_text - high)
        total = jnp.sum(p_own + p_text, axis=1, keepdims=True)
        acc = dot(p_own.astype(BF), kv[1, :, cols]) + dot(p_text.astype(BF), tv[:, cols])
        rows = slice(head * TEXT, (head + 1) * TEXT)
        acc_s[rows, :] = acc.astype(BF)
        high_s[rows, :] = jnp.broadcast_to(high, (TEXT, HEAD_DIM))
        total_s[rows, :] = jnp.broadcast_to(total, (TEXT, HEAD_DIM))

    for rank in range(PLANE):
        rows = slice(rank * EACH, (rank + 1) * EACH)
        out[rank, :EACH] = acc_s[rows, :]
        out[rank, EACH:] = stat_rows((high_s[rows, :], *split(total_s[rows, :])))
    onward.wait()


WHOLE = pl.BlockSpec(memory_space=pltpu.VMEM)
SCALARS = pl.BlockSpec(memory_space=pltpu.SMEM)
FAR = pl.BlockSpec(memory_space=pltpu.HBM)
ANY = pl.BlockSpec(memory_space=pl.ANY)


def text_part(pos, valid, tq, kv, tk, tv, w):
    count = HEADS_HERE * TEXT
    return pl.pallas_call(
        text_part_kernel,
        in_specs=[SCALARS, WHOLE, FAR, FAR, FAR, FAR, FAR],
        out_specs=(WHOLE, FAR),
        out_shape=(
            jax.ShapeDtypeStruct((PLANE, SLOT, HEAD_DIM), BF),
            jax.ShapeDtypeStruct(w.shape, BF),
        ),
        scratch_shapes=[pltpu.VMEM(x.shape, BF) for x in (tq, kv, tk, tv, w)]
        + [pltpu.VMEM((count, HEAD_DIM), t) for t in (BF, F32, F32)]
        + [pltpu.SemaphoreType.DMA((2, 4)), pltpu.SemaphoreType.DMA((2,))],
        cost_estimate=pl.CostEstimate(
            flops=5 * 10**9, bytes_accessed=2 << 20, transcendentals=10**6
        ),
        compiler_params=pltpu.CompilerParams(vmem_limit_bytes=VMEM),
        name="text_part",
    )(pos, valid, tq, kv, tk, tv, w)


def merge_kernel(parts, own, z_low, z_high, out, low, high, held, sems):
    inward, outward = [], []
    for j, ref in enumerate((z_low, own, z_high)):
        for side, target in enumerate((low, high)):
            part = ref.at[:, pl.ds((1 - side) * PAIR, PAIR), :]
            inward.append(pltpu.make_async_copy(part, held.at[j, side], sems.at[0, j, side]))
            outward.append(
                pltpu.make_async_copy(held.at[j, side], target.at[j], sems.at[1, j, side])
            )
    for copy in inward:
        copy.start()

    def between():
        for copy, onward in zip(inward, outward):
            copy.wait()
            onward.start()

    combine_kernel(1, parts, out, between=between)
    wait_all(outward)


def merge(parts, copies, own, z_low, z_high):
    shape = jax.ShapeDtypeStruct((3, 2, PAIR, WIDTH), BF)
    return pl.pallas_call(
        merge_kernel,
        in_specs=[WHOLE] + [ANY] * 3,
        out_specs=(WHOLE, ANY, ANY),
        out_shape=(jax.ShapeDtypeStruct((copies, SLOT, HEAD_DIM), BF), shape, shape),
        scratch_shapes=[
            pltpu.VMEM((3, 2, 2, PAIR, WIDTH), BF),
            pltpu.SemaphoreType.DMA((2, 3, 2)),
        ],
        cost_estimate=pl.CostEstimate(
            flops=2 * 10**9, bytes_accessed=6 << 20, transcendentals=0
        ),
        compiler_params=pltpu.CompilerParams(vmem_limit_bytes=24 << 20),
        name="text_merge",
    )(parts, own, z_low, z_high)


def combine_kernel(count, *refs, between=lambda: None):
    ins, out = refs[:count], refs[-1]
    parts = [ref.at[i] for ref in ins for i in range(ref.shape[0])]
    stats = [part[EACH:].astype(F32) for part in parts]
    highs = [s[0:1] for s in stats]
    high = functools.reduce(jnp.maximum, highs)
    weights = [jnp.exp2(h - high) for h in highs]
    total = sum(w * (s[1:2] + s[2:3]) for w, s in zip(weights, stats))
    finish = out.shape[1] == EACH
    if finish:
        lane = lax.broadcasted_iota(jnp.int32, (1, HEAD_DIM), 1)
        total = jnp.where(lane < EACH, total, 1.0)
        weights = [w / total for w in weights]
    row = lax.broadcasted_iota(jnp.int32, (HEAD_DIM, HEAD_DIM), 0)
    table = jnp.zeros((HEAD_DIM, HEAD_DIM), F32)
    for i, w in enumerate(weights):
        table = jnp.where(row == i, w, table)
    table = table.T
    between()
    sums = jnp.zeros((EACH, HEAD_DIM), F32)
    for i, part in enumerate(parts):
        sums += table[:EACH, i : i + 1] * part[:EACH].astype(F32)
    sums = sums.astype(BF)
    for at in range(out.shape[0]):
        out[at, :EACH] = sums
    if not finish:
        lines = lay_out((high, *split(total)))
        for at in range(out.shape[0]):
            out[at, EACH:] = lines


def combine(parts, copies, finish, name, *after):
    return pl.pallas_call(
        functools.partial(combine_kernel, len(parts)),
        in_specs=[WHOLE] * len(parts) + [ANY] * len(after),
        out_specs=WHOLE,
        out_shape=jax.ShapeDtypeStruct((copies, EACH if finish else SLOT, HEAD_DIM), BF),
        cost_estimate=pl.CostEstimate(
            flops=10**9, bytes_accessed=1 << 20, transcendentals=0
        ),
        compiler_params=pltpu.CompilerParams(vmem_limit_bytes=16 << 20),
        name=name,
    )(*parts, *after)


def halves_kernel(low, high, after, low_out, high_out, held, sems):
    half = low_out.shape[0]
    inward = [
        pltpu.make_async_copy(ref, held.at[i], sems.at[0, i])
        for i, ref in enumerate((low.at[0:half], high.at[half : 2 * half]))
    ]
    onward = [
        pltpu.make_async_copy(held.at[i], out, sems.at[1, i])
        for i, out in enumerate((low_out, high_out))
    ]
    for copy in inward:
        copy.start()
    for copy, following in zip(inward, onward):
        copy.wait()
        following.start()
    wait_all(onward)


def halves(low, high, after):
    shape = (low.shape[0] // 2, low.shape[1])
    return pl.pallas_call(
        halves_kernel,
        in_specs=[ANY] * 3,
        out_specs=(ANY, ANY),
        out_shape=[jax.ShapeDtypeStruct(shape, BF)] * 2,
        scratch_shapes=[pltpu.VMEM((2, *shape), BF), pltpu.SemaphoreType.DMA((2, 2))],
        cost_estimate=pl.CostEstimate(flops=0, bytes_accessed=2 << 20, transcendentals=0),
        compiler_params=pltpu.CompilerParams(vmem_limit_bytes=16 << 20),
        name="halves",
    )(low, high, after)


def video_kernel(pos, mask, valid, *rest):
    far, out_h, near, out, bias_s, sems = rest[:8], rest[9], rest[10:18], *rest[18:]
    q, tk, tv, own, z_low, z_high, t_low, t_high = near
    pairs = list(zip(far, near))
    begun = fetch(pairs, sems.at[0], FIRST)
    later = fetch(pairs, sems.at[1], REST)
    fill_bias(pos, mask, bias_s)
    text_bias = jnp.where(valid[...] > 0, 0.0, LOW)
    for head in range(HEADS_HERE):
        if head == 0:
            wait_all(begun)
        elif head == 1:
            wait_all(later)
        cols = slice(head * HEAD_DIM, (head + 1) * HEAD_DIM)
        one_head(
            q.at[:, cols],
            tk.at[:, cols],
            tv.at[:, cols],
            [ref.at[:, :, cols] for ref in (z_low, own, z_high)],
            [ref.at[:, :, :, cols] for ref in (t_low, t_high)],
            text_bias,
            bias_s,
            out.at[:, cols],
        )
    copy = pltpu.make_async_copy(out, out_h, sems.at[0, 0])
    copy.start()
    copy.wait()


def fill_bias(pos, mask, bias_s):
    row = lax.broadcasted_iota(jnp.int32, (8, PAIR), 0)
    col = lax.broadcasted_iota(jnp.int32, (8, PAIR), 1)
    second_q = row >= TILE
    second_k = jnp.bitwise_and(col, 7) >= TILE
    for a in range(2):
        for i in range(3):
            for j in range(3):
                where_t = pos[0] * 2 + a + i - 1
                where_h = pos[1] + j - 1
                inside = (where_t >= 0) & (where_t < pos[3]) & (where_h >= 0) & (where_h < pos[4])
                base = 9 * i + 3 * j

                def one(c, k):
                    if base + k == 13:
                        return jnp.where(inside, 0.0, LOW)
                    ok = inside & (mask[(a * 2 + c) * 27 + base + k] > 0)
                    return jnp.where(ok, 0.0, LOW)

                low = jnp.where(second_k, one(0, 2), one(0, 1))
                high = jnp.where(second_k, one(1, 1), one(1, 0))
                bias_s[a, i, j] = jnp.where(second_q, high, low)


def one_head(q, tk, tv, mids, sides, text_bias, bias_s, out):
    def rows(part):
        return (
            jnp.concatenate([sides[0][j, part] for j in range(3)], axis=0),
            jnp.concatenate(
                [ref[part, a * PAIR : (a + 1) * PAIR, :] for a in range(2) for ref in mids],
                axis=0,
            ),
            jnp.concatenate([sides[1][j, part] for j in range(3)], axis=0),
        )

    queries = q[...]
    k_low, k_mid, k_high = rows(0)
    v_low, v_mid, v_high = rows(1)
    s_mid = dot_t(queries, k_mid)
    s_text = dot_t(queries, tk[...])
    s_sides = (dot_t(queries[:PAIR], k_low), dot_t(queries[PAIR:], k_high))
    v_sides = (v_low, v_high)
    for a in range(2):
        mine = slice(a * PAIR, (a + 1) * PAIR)
        pieces = []
        for i in range(3):
            for j in range(3):
                at = (a + i - 1) * 3 + j
                if 0 <= a + i - 1 <= 1:
                    piece = s_mid[mine, at * PAIR : (at + 1) * PAIR]
                else:
                    piece = s_sides[a][:, j * PAIR : (j + 1) * PAIR]
                piece = piece.reshape(PAIR // 8, 8, PAIR) * SCALE2 + bias_s[a, i, j][None]
                pieces.append(piece.reshape(PAIR, PAIR))
        text_piece = s_text[mine] * SCALE2 + text_bias
        pieces.append(text_piece[:, :PAIR])
        pieces.append(text_piece[:, PAIR:])
        high = functools.reduce(jnp.maximum, pieces)
        high = jnp.max(high, axis=1, keepdims=True)
        weights = [jnp.exp2(piece - high) for piece in pieces]
        total = jnp.sum(functools.reduce(jnp.add, weights), axis=1, keepdims=True)
        weights = [w.astype(BF) for w in weights]
        side = weights[:3] if a == 0 else weights[6:9]
        mid = weights[3:9] if a == 0 else weights[:6]
        mixed = (
            dot(jnp.concatenate(side, axis=1), v_sides[a])
            + dot(jnp.concatenate(mid, axis=1), v_mid)
            + dot(jnp.concatenate(weights[9:], axis=1), tv[...])
        )
        out[mine, :] = (mixed / total).astype(BF)


def video_attention(pos, mask, valid, *arrays):
    return pl.pallas_call(
        video_kernel,
        in_specs=[SCALARS, SCALARS, WHOLE] + [FAR] * 4 + [ANY] * (len(arrays) - 4),
        out_specs=FAR,
        out_shape=jax.ShapeDtypeStruct((OWN, WIDTH), BF),
        scratch_shapes=[pltpu.VMEM(x.shape, BF) for x in arrays[:8]]
        + [pltpu.VMEM((OWN, WIDTH), BF), pltpu.VMEM((2, 3, 3, 8, PAIR), F32), pltpu.SemaphoreType.DMA((2, 8))],
        cost_estimate=pl.CostEstimate(
            flops=9 * 10**9, bytes_accessed=6 << 20, transcendentals=2 * 10**6
        ),
        compiler_params=pltpu.CompilerParams(vmem_limit_bytes=VMEM),
        name="video_attention",
    )(pos, mask, valid, *arrays)


def project(pos, near, mine, held, sems, read, put, out, sent, out_sems):
    width = held.shape[1] // 4
    for step, ref in zip((0, 1, 2, 3, 5, 6, 7), near):
        column = jnp.bitwise_and(pos[1] + step, 7)
        is_mine = lax.shift_right_logical(column, 2) == pos[2]
        slot = jnp.bitwise_and(column, 3)
        columns = pl.ds(pl.multiple_of(slot * width, width), width)

        @pl.when(is_mine if mine else jnp.logical_not(is_mine))
        def _():
            pltpu.make_async_copy(ref, held.at[:, columns], sems.at[slot]).start()

    column = jnp.bitwise_and(pos[1] + 4, 7)
    is_mine = lax.shift_right_logical(column, 2) == pos[2]
    late = is_mine if mine else jnp.logical_not(is_mine)
    late_slot = jnp.bitwise_and(column, 3)
    left = read()
    copies = []
    for pair in range(2):
        for slot in (2 * pair, 2 * pair + 1):
            columns = slice(slot * width, (slot + 1) * width)

            @pl.when(jnp.logical_not(late & (late_slot == slot)))
            def _():
                pltpu.make_async_copy(near[0], held.at[:, columns], sems.at[slot]).wait()

        columns = slice(2 * pair * width, 2 * (pair + 1) * width)
        sent[:, columns] = put(columns, dot(left, held[:, columns])).astype(BF)
        copies.append(
            pltpu.make_async_copy(sent.at[:, columns], out.at[:, columns], out_sems.at[pair])
        )
        copies[-1].start()
    wait_all(copies)


def by_head(parts):
    flat = parts.reshape(HEADS_HERE * TEXT, HEAD_DIM)
    heads = [flat[head * TEXT : (head + 1) * TEXT] for head in range(HEADS_HERE)]
    return jnp.concatenate(heads, axis=1)


def text_share_kernel(pos, parts_h, *rest):
    blocks, rest = rest[:7], rest[8:]
    rows_h, share, parts, rows, in_sems, held, sent, sems, out_sems = rest
    rows_copy = pltpu.make_async_copy(rows, rows_h, in_sems.at[1])
    copy = pltpu.make_async_copy(parts_h, parts, in_sems.at[0])
    copy.start()

    def read():
        copy.wait()
        rows[...] = by_head(parts[...])
        rows_copy.start()
        return rows[...]

    project(pos, blocks, False, held, sems, read, lambda _, x: x, share, sent, out_sems)
    rows_copy.wait()


def share_kernel(pos, rows_h, *rest):
    blocks, rest = rest[:7], rest[7:]
    share, rows, in_sems, held, sent, sems, out_sems = rest
    copy = pltpu.make_async_copy(rows_h, rows, in_sems.at[0])
    copy.start()

    def read():
        copy.wait()
        return rows[...]

    project(pos, blocks, False, held, sems, read, lambda _, x: x, share, sent, out_sems)


def finish_kernel(pos, rows_h, other_h, *rest):
    blocks, rest = rest[:7], rest[7:]
    out, rows, other, in_sems, held, sent, sems, out_sems = rest
    copies = [
        pltpu.make_async_copy(rows_h, rows, in_sems.at[0]),
        pltpu.make_async_copy(other_h, other, in_sems.at[1]),
    ]
    for copy in copies:
        copy.start()

    def read():
        wait_all(copies)
        return rows[...]

    def put(columns, terms):
        return terms + other[:, columns].astype(F32)

    project(pos, blocks, True, held, sems, read, put, out, sent, out_sems)


def project_call(kernel, name, pos, left, blocks, out_shape, out_specs, scratch, after=()):
    depth, width = blocks[0].shape
    return pl.pallas_call(
        kernel,
        in_specs=[SCALARS] + [FAR] + [ANY] * (len(left) - 1) + [FAR] * 7 + [ANY] * len(after),
        out_specs=out_specs,
        out_shape=out_shape,
        scratch_shapes=[pltpu.VMEM(x.shape, BF) for x in left]
        + scratch
        + [
            pltpu.SemaphoreType.DMA((2,)),
            pltpu.VMEM((depth, 4 * width), BF),
            pltpu.VMEM((TEXT, 4 * width), BF),
            pltpu.SemaphoreType.DMA((4,)),
            pltpu.SemaphoreType.DMA((2,)),
        ],
        cost_estimate=pl.CostEstimate(
            flops=8 * TEXT * depth * width, bytes_accessed=4 << 20, transcendentals=0
        ),
        compiler_params=pltpu.CompilerParams(vmem_limit_bytes=24 << 20),
        name=name,
    )(pos, *left, *blocks, *after)


def far_kernel(video_h, parts_h, top_h, bottom_h, terms, share, rows, parts, w, sems):
    half = top_h.shape[0]
    copies = [
        pltpu.make_async_copy(source, target, sems.at[i])
        for i, (source, target) in enumerate(
            (
                (video_h, rows.at[0:OWN]),
                (parts_h, parts),
                (top_h, w.at[0:half]),
                (bottom_h, w.at[half : 2 * half]),
            )
        )
    ]
    for copy in copies:
        copy.start()
    wait_all(copies)
    rows[OWN : OWN + TEXT] = by_head(parts[...])
    terms[...] = dot(rows[...], w[...])
    share[...] = terms[...].astype(BF)


def far_terms(video, parts, top, bottom):
    shape, depth, width = (OWN + TEXT, top.shape[1]), 2 * top.shape[0], top.shape[1]
    return pl.pallas_call(
        far_kernel,
        in_specs=[ANY] * 4,
        out_specs=(WHOLE, WHOLE),
        out_shape=(jax.ShapeDtypeStruct(shape, F32), jax.ShapeDtypeStruct(shape, BF)),
        scratch_shapes=[
            pltpu.VMEM((OWN + TEXT, depth), BF),
            pltpu.VMEM(parts.shape, BF),
            pltpu.VMEM((depth, width), BF),
            pltpu.SemaphoreType.DMA((4,)),
        ],
        cost_estimate=pl.CostEstimate(
            flops=2 * shape[0] * depth * width, bytes_accessed=4 << 20, transcendentals=0
        ),
        compiler_params=pltpu.CompilerParams(vmem_limit_bytes=24 << 20),
        name="far_terms",
    )(video, parts, top, bottom)


def last_kernel(pos, terms_h, other_h, video_in, text_in, video, text, terms, other, done, sems):
    width = terms.shape[1]
    column = jnp.bitwise_and(pos[1] + 4, 7)
    slot = jnp.bitwise_and(column, 3)
    columns = pl.ds(pl.multiple_of(slot * width, width), width)

    @pl.when(lax.shift_right_logical(column, 2) == pos[2])
    def _():
        copies = [
            pltpu.make_async_copy(terms_h, terms, sems.at[0]),
            pltpu.make_async_copy(other_h, other, sems.at[1]),
        ]
        for copy in copies:
            copy.start()
        wait_all(copies)
        done[...] = (terms[...] + other[...].astype(F32)).astype(BF)
        copies = [
            pltpu.make_async_copy(done.at[0:OWN], video.at[:, columns], sems.at[2]),
            pltpu.make_async_copy(done.at[OWN : OWN + TEXT], text.at[:, columns], sems.at[3]),
        ]
        for copy in copies:
            copy.start()
        wait_all(copies)


def last_columns(pos, terms, other, video, text):
    return pl.pallas_call(
        last_kernel,
        in_specs=[SCALARS] + [ANY] * 4,
        out_specs=(ANY, ANY),
        out_shape=[jax.ShapeDtypeStruct(x.shape, BF) for x in (video, text)],
        input_output_aliases={3: 0, 4: 1},
        scratch_shapes=[
            pltpu.VMEM(terms.shape, F32),
            pltpu.VMEM(terms.shape, BF),
            pltpu.VMEM(terms.shape, BF),
            pltpu.SemaphoreType.DMA((4,)),
        ],
        cost_estimate=pl.CostEstimate(flops=0, bytes_accessed=3 << 20, transcendentals=0),
        compiler_params=pltpu.CompilerParams(vmem_limit_bytes=24 << 20),
        name="last_columns",
    )(pos, terms, other, video, text)


def shards(video_q, video_kv, text_q, text_k, text_v, tile_mask, text_valid, w_out):
    frames, rows, cols, width = video_q.shape
    t_count, h_count = lax.axis_size("tm"), lax.axis_size("height")
    zero = jnp.int32(0)
    pos = jnp.stack(
        [
            lax.axis_index("tm"),
            lax.axis_index("height"),
            lax.axis_index("head"),
            zero + t_count * 2,
            zero + h_count,
        ]
    ).astype(jnp.int32)
    mask = tile_mask.reshape(-1)
    valid = text_valid.reshape(1, TEXT)
    own = video_kv.reshape(2, OWN, width)
    q = video_q.reshape(OWN, width)

    def up(x, axis, by=1):
        n = lax.axis_size(axis)
        return lax.ppermute(x, axis, [(i, (i + by) % n) for i in range(n)])

    def down(x, axis, by=1):
        return up(x, axis, -by)

    z_low, z_high = up(own, "height"), down(own, "height")
    parts, ring = text_part(pos, valid, text_q, own, text_k, text_v, w_out)
    before, after = [up(ring, "height")], [down(ring, "height")]
    parts = lax.all_to_all(parts, "tm", 0, 0, tiled=True)
    parts, low, high = merge(parts, h_count, own, z_low, z_high)
    t_low, t_high = up(low, "tm"), down(high, "tm")

    parts = lax.all_to_all(parts, "height", 0, 0, tiled=True)
    low, high = before[0], after[0]
    before.append(up(low, "height"))
    after.append(down(high, "height"))
    sums = combine([parts], t_count, True, "text_finish_sums")
    parts = lax.all_to_all(sums, "tm", 0, 0, tiled=True)
    low, high = before[1], after[1]
    before.append(up(low, "height"))
    after.append(down(high, "height"))
    video_rows = video_attention(
        pos, mask, valid, q, text_k, text_v, own, z_low, z_high, t_low, t_high, parts
    )
    low, high = halves(before[2], after[2], video_rows)
    far = [up(low, "height"), down(high, "height")]

    def swap(x):
        return lax.ppermute(x, "head", [(0, 1), (1, 0)])

    blocks = [w_out] + after + before[::-1]
    full = jax.ShapeDtypeStruct((OWN, 4 * w_out.shape[1]), BF)
    video_other = swap(
        project_call(share_kernel, "video_share", pos, [video_rows], blocks, full, FAR, [])
    )
    terms, share = far_terms(video_rows, parts, *far)
    text_rows, text_other = project_call(
        text_share_kernel,
        "text_share",
        pos,
        [parts],
        blocks,
        (jax.ShapeDtypeStruct((TEXT, WIDTH), BF), full),
        (FAR, FAR),
        [pltpu.VMEM((TEXT, WIDTH), BF)],
        [terms],
    )
    text_other = swap(text_other)
    video_out = project_call(
        finish_kernel, "video_finish", pos, [video_rows, video_other], blocks, full, FAR, []
    )
    text_out = project_call(
        finish_kernel, "text_finish", pos, [text_rows, text_other], blocks, full, FAR, []
    )
    video_out, text_out = last_columns(pos, terms, swap(share), video_out, text_out)
    return video_out.reshape(frames, rows, cols, -1), text_out


def solution(mesh):
    return jax.shard_map(
        shards,
        mesh=mesh,
        in_specs=(
            P("tm", "height", None, "head"),
            P(None, "tm", "height", None, "head"),
            P(None, "head"),
            P(None, "head"),
            P(None, "head"),
            P("tm", "height", None, None),
            P(),
            P("head", "height"),
        ),
        out_specs=(P("tm", "height", None, "head"), P(None, "head")),
        check_vma=False,
    )
```

```python
import functools

import jax
import jax.numpy as jnp
from jax import lax
from jax.experimental import pallas as pl
from jax.experimental.pallas import tpu as pltpu
from jax.sharding import PartitionSpec as P

HEAD_DIM = 128
TILE = 4
HEADS_HERE = 6
PAIR = 128
OWN = 256
TEXT = 256
WIDTH = HEADS_HERE * HEAD_DIM
PLANE = 16
EACH = HEADS_HERE * TEXT // PLANE
SLOT = 112
SCALE2 = HEAD_DIM ** (-0.5) * 1.4426950408889634
LOW = -1e30
VMEM = 60 << 20
BF = jnp.bfloat16
F32 = jnp.float32


def dot_t(a, b):
    return lax.dot_general(a, b, (((1,), (1,)), ((), ())), preferred_element_type=F32)


def dot(a, b):
    return jnp.dot(a, b, preferred_element_type=F32)


def fetch(pairs, sems, columns):
    copies = []
    for at, (source, target) in enumerate(pairs):
        where = (slice(None),) * (len(source.shape) - 1) + (columns,)
        copies.append(pltpu.make_async_copy(source.at[where], target.at[where], sems.at[at]))
    for copy in copies:
        copy.start()
    return copies


def wait_all(copies):
    for copy in copies:
        copy.wait()


FIRST, REST = slice(0, HEAD_DIM), slice(HEAD_DIM, WIDTH)


def stat_rows(values):
    row = lax.broadcasted_iota(jnp.int32, (EACH, HEAD_DIM), 0)
    col = lax.broadcasted_iota(jnp.int32, (EACH, HEAD_DIM), 1)
    lines = [jnp.sum(jnp.where(row == col, v, 0.0), axis=0, keepdims=True) for v in values]
    return lay_out(lines)


def lay_out(lines):
    row = lax.broadcasted_iota(jnp.int32, (SLOT - EACH, HEAD_DIM), 0)
    full = jnp.zeros((SLOT - EACH, HEAD_DIM), F32)
    for at, line in enumerate(lines):
        full = jnp.where(row == at, line, full)
    return full.astype(BF)


def split(total):
    high = total.astype(BF).astype(F32)
    return high, total - high


def text_part_kernel(
    pos, valid, tq_h, kv_h, tk_h, tv_h, w_h, out, w_out, tq, kv, tk, tv, w, acc_s, high_s, total_s, sems, w_sems
):
    inward = pltpu.make_async_copy(w_h, w, w_sems.at[0])
    onward = pltpu.make_async_copy(w, w_out, w_sems.at[1])
    pairs = [(tq_h, tq), (kv_h, kv), (tk_h, tk), (tv_h, tv)]
    begun = fetch(pairs, sems.at[0], FIRST)
    later = fetch(pairs, sems.at[1], REST)
    inward.start()
    first = (pos[0] == 0) & (pos[1] == 0)
    bias = jnp.where((valid[...] > 0) & first, 0.0, LOW)
    for head in range(HEADS_HERE):
        if head == 0:
            wait_all(begun)
        elif head == 1:
            wait_all(later)
            inward.wait()
            onward.start()
        cols = slice(head * HEAD_DIM, (head + 1) * HEAD_DIM)
        q = tq[:, cols]
        s_own = dot_t(q, kv[0, :, cols]) * SCALE2
        s_text = dot_t(q, tk[:, cols]) * SCALE2 + bias
        high = jnp.max(jnp.maximum(s_own, s_text), axis=1, keepdims=True)
        high = high.astype(BF).astype(F32)
        p_own = jnp.exp2(s_own - high)
        p_text = jnp.exp2(s_text - high)
        total = jnp.sum(p_own + p_text, axis=1, keepdims=True)
        acc = dot(p_own.astype(BF), kv[1, :, cols]) + dot(p_text.astype(BF), tv[:, cols])
        rows = slice(head * TEXT, (head + 1) * TEXT)
        acc_s[rows, :] = acc.astype(BF)
        high_s[rows, :] = jnp.broadcast_to(high, (TEXT, HEAD_DIM))
        total_s[rows, :] = jnp.broadcast_to(total, (TEXT, HEAD_DIM))

    for rank in range(PLANE):
        rows = slice(rank * EACH, (rank + 1) * EACH)
        out[rank, :EACH] = acc_s[rows, :]
        out[rank, EACH:] = stat_rows((high_s[rows, :], *split(total_s[rows, :])))
    onward.wait()


WHOLE = pl.BlockSpec(memory_space=pltpu.VMEM)
SCALARS = pl.BlockSpec(memory_space=pltpu.SMEM)
FAR = pl.BlockSpec(memory_space=pltpu.HBM)
ANY = pl.BlockSpec(memory_space=pl.ANY)


def text_part(pos, valid, tq, kv, tk, tv, w):
    count = HEADS_HERE * TEXT
    return pl.pallas_call(
        text_part_kernel,
        in_specs=[SCALARS, WHOLE, FAR, FAR, FAR, FAR, FAR],
        out_specs=(WHOLE, FAR),
        out_shape=(
            jax.ShapeDtypeStruct((PLANE, SLOT, HEAD_DIM), BF),
            jax.ShapeDtypeStruct(w.shape, BF),
        ),
        scratch_shapes=[pltpu.VMEM(x.shape, BF) for x in (tq, kv, tk, tv, w)]
        + [pltpu.VMEM((count, HEAD_DIM), t) for t in (BF, F32, F32)]
        + [pltpu.SemaphoreType.DMA((2, 4)), pltpu.SemaphoreType.DMA((2,))],
        cost_estimate=pl.CostEstimate(
            flops=5 * 10**9, bytes_accessed=2 << 20, transcendentals=10**6
        ),
        compiler_params=pltpu.CompilerParams(vmem_limit_bytes=VMEM),
        name="text_part",
    )(pos, valid, tq, kv, tk, tv, w)


def merge_kernel(parts, own, z_low, z_high, out, low, high, held, sems):
    inward, outward = [], []
    for j, ref in enumerate((z_low, own, z_high)):
        for side, target in enumerate((low, high)):
            part = ref.at[:, pl.ds((1 - side) * PAIR, PAIR), :]
            inward.append(pltpu.make_async_copy(part, held.at[j, side], sems.at[0, j, side]))
            outward.append(
                pltpu.make_async_copy(held.at[j, side], target.at[j], sems.at[1, j, side])
            )
    for copy in inward:
        copy.start()

    def between():
        for copy, onward in zip(inward, outward):
            copy.wait()
            onward.start()

    combine_kernel(1, parts, out, between=between)
    wait_all(outward)


def merge(parts, copies, own, z_low, z_high):
    shape = jax.ShapeDtypeStruct((3, 2, PAIR, WIDTH), BF)
    return pl.pallas_call(
        merge_kernel,
        in_specs=[WHOLE] + [ANY] * 3,
        out_specs=(WHOLE, ANY, ANY),
        out_shape=(jax.ShapeDtypeStruct((copies, SLOT, HEAD_DIM), BF), shape, shape),
        scratch_shapes=[
            pltpu.VMEM((3, 2, 2, PAIR, WIDTH), BF),
            pltpu.SemaphoreType.DMA((2, 3, 2)),
        ],
        cost_estimate=pl.CostEstimate(
            flops=2 * 10**9, bytes_accessed=6 << 20, transcendentals=0
        ),
        compiler_params=pltpu.CompilerParams(vmem_limit_bytes=24 << 20),
        name="text_merge",
    )(parts, own, z_low, z_high)


def combine_kernel(count, *refs, between=lambda: None):
    ins, out = refs[:count], refs[-1]
    parts = [ref.at[i] for ref in ins for i in range(ref.shape[0])]
    stats = [part[EACH:].astype(F32) for part in parts]
    highs = [s[0:1] for s in stats]
    high = functools.reduce(jnp.maximum, highs)
    weights = [jnp.exp2(h - high) for h in highs]
    total = sum(w * (s[1:2] + s[2:3]) for w, s in zip(weights, stats))
    finish = out.shape[1] == EACH
    if finish:
        lane = lax.broadcasted_iota(jnp.int32, (1, HEAD_DIM), 1)
        total = jnp.where(lane < EACH, total, 1.0)
        weights = [w / total for w in weights]
    row = lax.broadcasted_iota(jnp.int32, (HEAD_DIM, HEAD_DIM), 0)
    table = jnp.zeros((HEAD_DIM, HEAD_DIM), F32)
    for i, w in enumerate(weights):
        table = jnp.where(row == i, w, table)
    table = table.T
    between()
    sums = jnp.zeros((EACH, HEAD_DIM), F32)
    for i, part in enumerate(parts):
        sums += table[:EACH, i : i + 1] * part[:EACH].astype(F32)
    sums = sums.astype(BF)
    for at in range(out.shape[0]):
        out[at, :EACH] = sums
    if not finish:
        lines = lay_out((high, *split(total)))
        for at in range(out.shape[0]):
            out[at, EACH:] = lines


def combine(parts, copies, finish, name, *after):
    return pl.pallas_call(
        functools.partial(combine_kernel, len(parts)),
        in_specs=[WHOLE] * len(parts) + [ANY] * len(after),
        out_specs=WHOLE,
        out_shape=jax.ShapeDtypeStruct((copies, EACH if finish else SLOT, HEAD_DIM), BF),
        cost_estimate=pl.CostEstimate(
            flops=10**9, bytes_accessed=1 << 20, transcendentals=0
        ),
        compiler_params=pltpu.CompilerParams(vmem_limit_bytes=16 << 20),
        name=name,
    )(*parts, *after)


def halves_kernel(low, high, after, low_out, high_out, held, sems):
    half = low_out.shape[0]
    inward = [
        pltpu.make_async_copy(ref, held.at[i], sems.at[0, i])
        for i, ref in enumerate((low.at[0:half], high.at[half : 2 * half]))
    ]
    onward = [
        pltpu.make_async_copy(held.at[i], out, sems.at[1, i])
        for i, out in enumerate((low_out, high_out))
    ]
    for copy in inward:
        copy.start()
    for copy, following in zip(inward, onward):
        copy.wait()
        following.start()
    wait_all(onward)


def halves(low, high, after):
    shape = (low.shape[0] // 2, low.shape[1])
    return pl.pallas_call(
        halves_kernel,
        in_specs=[ANY] * 3,
        out_specs=(ANY, ANY),
        out_shape=[jax.ShapeDtypeStruct(shape, BF)] * 2,
        scratch_shapes=[pltpu.VMEM((2, *shape), BF), pltpu.SemaphoreType.DMA((2, 2))],
        cost_estimate=pl.CostEstimate(flops=0, bytes_accessed=2 << 20, transcendentals=0),
        compiler_params=pltpu.CompilerParams(vmem_limit_bytes=16 << 20),
        name="halves",
    )(low, high, after)


def video_kernel(pos, mask, valid, *rest):
    far, out_h, near, out, bias_s, sems = rest[:8], rest[9], rest[10:18], *rest[18:]
    q, tk, tv, own, z_low, z_high, t_low, t_high = near
    pairs = list(zip(far, near))
    begun = fetch(pairs, sems.at[0], FIRST)
    later = fetch(pairs, sems.at[1], REST)
    fill_bias(pos, mask, bias_s)
    text_bias = jnp.where(valid[...] > 0, 0.0, LOW)
    for head in range(HEADS_HERE):
        if head == 0:
            wait_all(begun)
        elif head == 1:
            wait_all(later)
        cols = slice(head * HEAD_DIM, (head + 1) * HEAD_DIM)
        one_head(
            q.at[:, cols],
            tk.at[:, cols],
            tv.at[:, cols],
            [ref.at[:, :, cols] for ref in (z_low, own, z_high)],
            [ref.at[:, :, :, cols] for ref in (t_low, t_high)],
            text_bias,
            bias_s,
            out.at[:, cols],
        )
    copy = pltpu.make_async_copy(out, out_h, sems.at[0, 0])
    copy.start()
    copy.wait()


def fill_bias(pos, mask, bias_s):
    row = lax.broadcasted_iota(jnp.int32, (8, PAIR), 0)
    col = lax.broadcasted_iota(jnp.int32, (8, PAIR), 1)
    second_q = row >= TILE
    second_k = jnp.bitwise_and(col, 7) >= TILE
    for a in range(2):
        for i in range(3):
            for j in range(3):
                where_t = pos[0] * 2 + a + i - 1
                where_h = pos[1] + j - 1
                inside = (where_t >= 0) & (where_t < pos[3]) & (where_h >= 0) & (where_h < pos[4])
                base = 9 * i + 3 * j

                def one(c, k):
                    if base + k == 13:
                        return jnp.where(inside, 0.0, LOW)
                    ok = inside & (mask[(a * 2 + c) * 27 + base + k] > 0)
                    return jnp.where(ok, 0.0, LOW)

                low = jnp.where(second_k, one(0, 2), one(0, 1))
                high = jnp.where(second_k, one(1, 1), one(1, 0))
                bias_s[a, i, j] = jnp.where(second_q, high, low)


def one_head(q, tk, tv, mids, sides, text_bias, bias_s, out):
    def rows(part):
        return (
            jnp.concatenate([sides[0][j, part] for j in range(3)], axis=0),
            jnp.concatenate(
                [ref[part, a * PAIR : (a + 1) * PAIR, :] for a in range(2) for ref in mids],
                axis=0,
            ),
            jnp.concatenate([sides[1][j, part] for j in range(3)], axis=0),
        )

    queries = q[...]
    k_low, k_mid, k_high = rows(0)
    v_low, v_mid, v_high = rows(1)
    s_mid = dot_t(queries, k_mid)
    s_text = dot_t(queries, tk[...])
    s_sides = (dot_t(queries[:PAIR], k_low), dot_t(queries[PAIR:], k_high))
    v_sides = (v_low, v_high)
    for a in range(2):
        mine = slice(a * PAIR, (a + 1) * PAIR)
        pieces = []
        for i in range(3):
            for j in range(3):
                at = (a + i - 1) * 3 + j
                if 0 <= a + i - 1 <= 1:
                    piece = s_mid[mine, at * PAIR : (at + 1) * PAIR]
                else:
                    piece = s_sides[a][:, j * PAIR : (j + 1) * PAIR]
                piece = piece.reshape(PAIR // 8, 8, PAIR) * SCALE2 + bias_s[a, i, j][None]
                pieces.append(piece.reshape(PAIR, PAIR))
        text_piece = s_text[mine] * SCALE2 + text_bias
        pieces.append(text_piece[:, :PAIR])
        pieces.append(text_piece[:, PAIR:])
        high = functools.reduce(jnp.maximum, pieces)
        high = jnp.max(high, axis=1, keepdims=True)
        weights = [jnp.exp2(piece - high) for piece in pieces]
        total = jnp.sum(functools.reduce(jnp.add, weights), axis=1, keepdims=True)
        weights = [w.astype(BF) for w in weights]
        side = weights[:3] if a == 0 else weights[6:9]
        mid = weights[3:9] if a == 0 else weights[:6]
        mixed = (
            dot(jnp.concatenate(side, axis=1), v_sides[a])
            + dot(jnp.concatenate(mid, axis=1), v_mid)
            + dot(jnp.concatenate(weights[9:], axis=1), tv[...])
        )
        out[mine, :] = (mixed / total).astype(BF)


def video_attention(pos, mask, valid, *arrays):
    return pl.pallas_call(
        video_kernel,
        in_specs=[SCALARS, SCALARS, WHOLE] + [FAR] * 4 + [ANY] * (len(arrays) - 4),
        out_specs=FAR,
        out_shape=jax.ShapeDtypeStruct((OWN, WIDTH), BF),
        scratch_shapes=[pltpu.VMEM(x.shape, BF) for x in arrays[:8]]
        + [pltpu.VMEM((OWN, WIDTH), BF), pltpu.VMEM((2, 3, 3, 8, PAIR), F32), pltpu.SemaphoreType.DMA((2, 8))],
        cost_estimate=pl.CostEstimate(
            flops=9 * 10**9, bytes_accessed=6 << 20, transcendentals=2 * 10**6
        ),
        compiler_params=pltpu.CompilerParams(vmem_limit_bytes=VMEM),
        name="video_attention",
    )(pos, mask, valid, *arrays)


def project(pos, near, mine, held, sems, read, put, out, sent, out_sems):
    width = held.shape[1] // 4
    for step, ref in zip((0, 1, 2, 3, 5, 6, 7), near):
        column = jnp.bitwise_and(pos[1] + step, 7)
        is_mine = lax.shift_right_logical(column, 2) == pos[2]
        slot = jnp.bitwise_and(column, 3)
        columns = pl.ds(pl.multiple_of(slot * width, width), width)

        @pl.when(is_mine if mine else jnp.logical_not(is_mine))
        def _():
            pltpu.make_async_copy(ref, held.at[:, columns], sems.at[slot]).start()

    column = jnp.bitwise_and(pos[1] + 4, 7)
    is_mine = lax.shift_right_logical(column, 2) == pos[2]
    late = is_mine if mine else jnp.logical_not(is_mine)
    late_slot = jnp.bitwise_and(column, 3)
    left = read()
    copies = []
    for pair in range(2):
        for slot in (2 * pair, 2 * pair + 1):
            columns = slice(slot * width, (slot + 1) * width)

            @pl.when(jnp.logical_not(late & (late_slot == slot)))
            def _():
                pltpu.make_async_copy(near[0], held.at[:, columns], sems.at[slot]).wait()

        columns = slice(2 * pair * width, 2 * (pair + 1) * width)
        sent[:, columns] = put(columns, dot(left, held[:, columns])).astype(BF)
        copies.append(
            pltpu.make_async_copy(sent.at[:, columns], out.at[:, columns], out_sems.at[pair])
        )
        copies[-1].start()
    wait_all(copies)


def by_head(parts):
    flat = parts.reshape(HEADS_HERE * TEXT, HEAD_DIM)
    heads = [flat[head * TEXT : (head + 1) * TEXT] for head in range(HEADS_HERE)]
    return jnp.concatenate(heads, axis=1)


def text_share_kernel(pos, parts_h, *rest):
    blocks, (video_h, top_h, bottom_h), rest = rest[:7], rest[7:10], rest[10:]
    rows_h, share, terms, far_share, parts, rows, video, w, far_sems, in_sems, *others = rest
    half = top_h.shape[0]
    rows_copy = pltpu.make_async_copy(rows, rows_h, in_sems.at[1])
    copy = pltpu.make_async_copy(parts_h, parts, in_sems.at[0])
    copy.start()
    copies = [
        pltpu.make_async_copy(video_h, video, far_sems.at[0]),
        pltpu.make_async_copy(top_h, w.at[0:half], far_sems.at[1]),
        pltpu.make_async_copy(bottom_h, w.at[half : 2 * half], far_sems.at[2]),
    ]
    for each in copies:
        each.start()

    def read():
        copy.wait()
        rows[...] = by_head(parts[...])
        rows_copy.start()
        wait_all(copies)
        for at, left in enumerate((video, rows)):
            part = slice(at * OWN, (at + 1) * OWN)
            terms[part, :] = dot(left[...], w[...])
            far_share[part, :] = terms[part, :].astype(BF)
        return rows[...]

    held, sent, sems, out_sems = others
    project(pos, blocks, False, held, sems, read, lambda _, x: x, share, sent, out_sems)
    rows_copy.wait()


def share_kernel(pos, rows_h, *rest):
    blocks, rest = rest[:7], rest[7:]
    share, rows, in_sems, held, sent, sems, out_sems = rest
    copy = pltpu.make_async_copy(rows_h, rows, in_sems.at[0])
    copy.start()

    def read():
        copy.wait()
        return rows[...]

    project(pos, blocks, False, held, sems, read, lambda _, x: x, share, sent, out_sems)


def finish_kernel(pos, rows_h, other_h, *rest):
    blocks, rest = rest[:7], rest[7:]
    out, rows, other, in_sems, held, sent, sems, out_sems = rest
    copies = [
        pltpu.make_async_copy(rows_h, rows, in_sems.at[0]),
        pltpu.make_async_copy(other_h, other, in_sems.at[1]),
    ]
    for copy in copies:
        copy.start()

    def read():
        wait_all(copies)
        return rows[...]

    def put(columns, terms):
        return terms + other[:, columns].astype(F32)

    project(pos, blocks, True, held, sems, read, put, out, sent, out_sems)


def project_call(kernel, name, pos, left, blocks, out_shape, out_specs, scratch, after=(), aliases=None):
    depth, width = blocks[0].shape
    return pl.pallas_call(
        kernel,
        in_specs=[SCALARS] + [FAR] + [ANY] * (len(left) - 1) + [FAR] * 7 + [ANY] * len(after),
        out_specs=out_specs,
        out_shape=out_shape,
        input_output_aliases=aliases or {},
        scratch_shapes=[pltpu.VMEM(x.shape, BF) for x in left]
        + scratch
        + [
            pltpu.SemaphoreType.DMA((2,)),
            pltpu.VMEM((depth, 4 * width), BF),
            pltpu.VMEM((TEXT, 4 * width), BF),
            pltpu.SemaphoreType.DMA((4,)),
            pltpu.SemaphoreType.DMA((2,)),
        ],
        cost_estimate=pl.CostEstimate(
            flops=8 * TEXT * depth * width, bytes_accessed=4 << 20, transcendentals=0
        ),
        compiler_params=pltpu.CompilerParams(vmem_limit_bytes=24 << 20),
        name=name,
    )(pos, *left, *blocks, *after)


def text_finish_kernel(pos, rows_h, other_h, *rest):
    blocks, (terms_h, far_h, _, out, video), rest = rest[:7], rest[7:12], rest[12:]
    rows, other, terms, far, done, far_sems, *others = rest
    width = terms.shape[1]
    column = jnp.bitwise_and(pos[1] + 4, 7)
    columns = pl.ds(pl.multiple_of(jnp.bitwise_and(column, 3) * width, width), width)
    is_mine = lax.shift_right_logical(column, 2) == pos[2]
    inward = [
        pltpu.make_async_copy(terms_h, terms, far_sems.at[0]),
        pltpu.make_async_copy(far_h, far, far_sems.at[1]),
    ]
    outward = [
        pltpu.make_async_copy(done.at[0:OWN], video.at[:, columns], far_sems.at[2]),
        pltpu.make_async_copy(done.at[OWN : OWN + TEXT], out.at[:, columns], far_sems.at[3]),
    ]

    @pl.when(is_mine)
    def _():
        for copy in inward:
            copy.start()

    finish_kernel(pos, rows_h, other_h, *blocks, out, rows, other, *others)

    @pl.when(is_mine)
    def _():
        wait_all(inward)
        done[...] = (terms[...] + far[...].astype(F32)).astype(BF)
        for copy in outward:
            copy.start()
        wait_all(outward)


def shards(video_q, video_kv, text_q, text_k, text_v, tile_mask, text_valid, w_out):
    frames, rows, cols, width = video_q.shape
    t_count, h_count = lax.axis_size("tm"), lax.axis_size("height")
    zero = jnp.int32(0)
    pos = jnp.stack(
        [
            lax.axis_index("tm"),
            lax.axis_index("height"),
            lax.axis_index("head"),
            zero + t_count * 2,
            zero + h_count,
        ]
    ).astype(jnp.int32)
    mask = tile_mask.reshape(-1)
    valid = text_valid.reshape(1, TEXT)
    own = video_kv.reshape(2, OWN, width)
    q = video_q.reshape(OWN, width)

    def up(x, axis, by=1):
        n = lax.axis_size(axis)
        return lax.ppermute(x, axis, [(i, (i + by) % n) for i in range(n)])

    def down(x, axis, by=1):
        return up(x, axis, -by)

    z_low, z_high = up(own, "height"), down(own, "height")
    parts, ring = text_part(pos, valid, text_q, own, text_k, text_v, w_out)
    before, after = [up(ring, "height")], [down(ring, "height")]
    parts = lax.all_to_all(parts, "tm", 0, 0, tiled=True)
    parts, low, high = merge(parts, h_count, own, z_low, z_high)
    t_low, t_high = up(low, "tm"), down(high, "tm")

    parts = lax.all_to_all(parts, "height", 0, 0, tiled=True)
    low, high = before[0], after[0]
    before.append(up(low, "height"))
    after.append(down(high, "height"))
    sums = combine([parts], t_count, True, "text_finish_sums")
    parts = lax.all_to_all(sums, "tm", 0, 0, tiled=True)
    low, high = before[1], after[1]
    before.append(up(low, "height"))
    after.append(down(high, "height"))
    video_rows = video_attention(
        pos, mask, valid, q, text_k, text_v, own, z_low, z_high, t_low, t_high, parts
    )
    low, high = halves(before[2], after[2], video_rows)
    far = [up(low, "height"), down(high, "height")]

    def swap(x):
        return lax.ppermute(x, "head", [(0, 1), (1, 0)])

    blocks = [w_out] + after + before[::-1]
    full = jax.ShapeDtypeStruct((OWN, 4 * w_out.shape[1]), BF)
    video_other = swap(
        project_call(share_kernel, "video_share", pos, [video_rows], blocks, full, FAR, [])
    )
    far_shape = (OWN + TEXT, w_out.shape[1])
    text_rows, text_other, terms, share = project_call(
        text_share_kernel,
        "text_share",
        pos,
        [parts],
        blocks,
        (
            jax.ShapeDtypeStruct((TEXT, WIDTH), BF),
            full,
            jax.ShapeDtypeStruct(far_shape, F32),
            jax.ShapeDtypeStruct(far_shape, BF),
        ),
        (FAR, FAR, WHOLE, WHOLE),
        [
            pltpu.VMEM((TEXT, WIDTH), BF),
            pltpu.VMEM((OWN, WIDTH), BF),
            pltpu.VMEM(w_out.shape, BF),
            pltpu.SemaphoreType.DMA((3,)),
        ],
        [video_rows, *far],
    )
    text_other = swap(text_other)
    video_out = project_call(
        finish_kernel, "video_finish", pos, [video_rows, video_other], blocks, full, FAR, []
    )
    text_out, video_out = project_call(
        text_finish_kernel,
        "text_finish",
        pos,
        [text_rows, text_other],
        blocks,
        (full, full),
        (FAR, ANY),
        [pltpu.VMEM(terms.shape, t) for t in (F32, BF, BF)] + [pltpu.SemaphoreType.DMA((4,))],
        [terms, swap(share), video_out],
        {12: 1},
    )
    return video_out.reshape(frames, rows, cols, -1), text_out


def solution(mesh):
    return jax.shard_map(
        shards,
        mesh=mesh,
        in_specs=(
            P("tm", "height", None, "head"),
            P(None, "tm", "height", None, "head"),
            P(None, "head"),
            P(None, "head"),
            P(None, "head"),
            P("tm", "height", None, None),
            P(),
            P("head", "height"),
        ),
        out_specs=(P("tm", "height", None, "head"), P(None, "head")),
        check_vma=False,
    )
```

```python
import functools

import jax
import jax.numpy as jnp
from jax import lax
from jax.experimental import pallas as pl
from jax.experimental.pallas import tpu as pltpu
from jax.sharding import PartitionSpec as P

HEAD_DIM = 128
TILE = 4
HEADS_HERE = 6
PAIR = 128
OWN = 256
TEXT = 256
WIDTH = HEADS_HERE * HEAD_DIM
PLANE = 16
EACH = HEADS_HERE * TEXT // PLANE
SLOT = 112
SCALE2 = HEAD_DIM ** (-0.5) * 1.4426950408889634
LOW = -1e30
VMEM = 60 << 20
BF = jnp.bfloat16
F32 = jnp.float32


def dot_t(a, b):
    return lax.dot_general(a, b, (((1,), (1,)), ((), ())), preferred_element_type=F32)


def dot(a, b):
    return jnp.dot(a, b, preferred_element_type=F32)


def fetch(pairs, sems, columns):
    copies = []
    for at, (source, target) in enumerate(pairs):
        where = (slice(None),) * (len(source.shape) - 1) + (columns,)
        copies.append(pltpu.make_async_copy(source.at[where], target.at[where], sems.at[at]))
    for copy in copies:
        copy.start()
    return copies


def wait_all(copies):
    for copy in copies:
        copy.wait()


FIRST, REST = slice(0, HEAD_DIM), slice(HEAD_DIM, WIDTH)


def stat_rows(values):
    row = lax.broadcasted_iota(jnp.int32, (EACH, HEAD_DIM), 0)
    col = lax.broadcasted_iota(jnp.int32, (EACH, HEAD_DIM), 1)
    lines = [jnp.sum(jnp.where(row == col, v, 0.0), axis=0, keepdims=True) for v in values]
    return lay_out(lines)


def lay_out(lines):
    row = lax.broadcasted_iota(jnp.int32, (SLOT - EACH, HEAD_DIM), 0)
    full = jnp.zeros((SLOT - EACH, HEAD_DIM), F32)
    for at, line in enumerate(lines):
        full = jnp.where(row == at, line, full)
    return full.astype(BF)


def split(total):
    high = total.astype(BF).astype(F32)
    return high, total - high


def text_part_kernel(
    pos, valid, tq_h, kv_h, tk_h, tv_h, w_h, out, w_out, tq, kv, tk, tv, w, acc_s, high_s, total_s, sems, w_sems
):
    inward = pltpu.make_async_copy(w_h, w, w_sems.at[0])
    onward = pltpu.make_async_copy(w, w_out, w_sems.at[1])
    pairs = [(tq_h, tq), (kv_h, kv), (tk_h, tk), (tv_h, tv)]
    begun = fetch(pairs, sems.at[0], FIRST)
    later = fetch(pairs, sems.at[1], REST)
    inward.start()
    first = (pos[0] == 0) & (pos[1] == 0)
    bias = jnp.where((valid[...] > 0) & first, 0.0, LOW)
    for head in range(HEADS_HERE):
        if head == 0:
            wait_all(begun)
        elif head == 1:
            wait_all(later)
            inward.wait()
            onward.start()
        cols = slice(head * HEAD_DIM, (head + 1) * HEAD_DIM)
        q = tq[:, cols]
        s_own = dot_t(q, kv[0, :, cols]) * SCALE2
        s_text = dot_t(q, tk[:, cols]) * SCALE2 + bias
        high = jnp.max(jnp.maximum(s_own, s_text), axis=1, keepdims=True)
        high = high.astype(BF).astype(F32)
        p_own = jnp.exp2(s_own - high)
        p_text = jnp.exp2(s_text - high)
        total = jnp.sum(p_own + p_text, axis=1, keepdims=True)
        acc = dot(p_own.astype(BF), kv[1, :, cols]) + dot(p_text.astype(BF), tv[:, cols])
        rows = slice(head * TEXT, (head + 1) * TEXT)
        acc_s[rows, :] = acc.astype(BF)
        high_s[rows, :] = jnp.broadcast_to(high, (TEXT, HEAD_DIM))
        total_s[rows, :] = jnp.broadcast_to(total, (TEXT, HEAD_DIM))

    for rank in range(PLANE):
        rows = slice(rank * EACH, (rank + 1) * EACH)
        out[rank, :EACH] = acc_s[rows, :]
        out[rank, EACH:] = stat_rows((high_s[rows, :], *split(total_s[rows, :])))
    onward.wait()


WHOLE = pl.BlockSpec(memory_space=pltpu.VMEM)
SCALARS = pl.BlockSpec(memory_space=pltpu.SMEM)
FAR = pl.BlockSpec(memory_space=pltpu.HBM)
ANY = pl.BlockSpec(memory_space=pl.ANY)


def text_part(pos, valid, tq, kv, tk, tv, w):
    count = HEADS_HERE * TEXT
    return pl.pallas_call(
        text_part_kernel,
        in_specs=[SCALARS, WHOLE, FAR, FAR, FAR, FAR, FAR],
        out_specs=(WHOLE, FAR),
        out_shape=(
            jax.ShapeDtypeStruct((PLANE, SLOT, HEAD_DIM), BF),
            jax.ShapeDtypeStruct(w.shape, BF),
        ),
        scratch_shapes=[pltpu.VMEM(x.shape, BF) for x in (tq, kv, tk, tv, w)]
        + [pltpu.VMEM((count, HEAD_DIM), t) for t in (BF, F32, F32)]
        + [pltpu.SemaphoreType.DMA((2, 4)), pltpu.SemaphoreType.DMA((2,))],
        cost_estimate=pl.CostEstimate(
            flops=5 * 10**9, bytes_accessed=2 << 20, transcendentals=10**6
        ),
        compiler_params=pltpu.CompilerParams(vmem_limit_bytes=VMEM),
        name="text_part",
    )(pos, valid, tq, kv, tk, tv, w)


def merge_kernel(parts, own, z_low, z_high, out, low, high, held, sems):
    inward, outward = [], []
    for j, ref in enumerate((z_low, own, z_high)):
        for side, target in enumerate((low, high)):
            part = ref.at[:, pl.ds((1 - side) * PAIR, PAIR), :]
            inward.append(pltpu.make_async_copy(part, held.at[j, side], sems.at[0, j, side]))
            outward.append(
                pltpu.make_async_copy(held.at[j, side], target.at[j], sems.at[1, j, side])
            )
    for copy in inward:
        copy.start()

    def between():
        for copy, onward in zip(inward, outward):
            copy.wait()
            onward.start()

    combine_kernel(1, parts, out, between=between)
    wait_all(outward)


def merge(parts, copies, own, z_low, z_high):
    shape = jax.ShapeDtypeStruct((3, 2, PAIR, WIDTH), BF)
    return pl.pallas_call(
        merge_kernel,
        in_specs=[WHOLE] + [ANY] * 3,
        out_specs=(WHOLE, ANY, ANY),
        out_shape=(jax.ShapeDtypeStruct((copies, SLOT, HEAD_DIM), BF), shape, shape),
        scratch_shapes=[
            pltpu.VMEM((3, 2, 2, PAIR, WIDTH), BF),
            pltpu.SemaphoreType.DMA((2, 3, 2)),
        ],
        cost_estimate=pl.CostEstimate(
            flops=2 * 10**9, bytes_accessed=6 << 20, transcendentals=0
        ),
        compiler_params=pltpu.CompilerParams(vmem_limit_bytes=24 << 20),
        name="text_merge",
    )(parts, own, z_low, z_high)


def combine_kernel(count, *refs, between=lambda: None):
    ins, out = refs[:count], refs[-1]
    parts = [ref.at[i] for ref in ins for i in range(ref.shape[0])]
    stats = [part[EACH:].astype(F32) for part in parts]
    highs = [s[0:1] for s in stats]
    high = functools.reduce(jnp.maximum, highs)
    weights = [jnp.exp2(h - high) for h in highs]
    total = sum(w * (s[1:2] + s[2:3]) for w, s in zip(weights, stats))
    finish = out.shape[1] == EACH
    if finish:
        lane = lax.broadcasted_iota(jnp.int32, (1, HEAD_DIM), 1)
        total = jnp.where(lane < EACH, total, 1.0)
        weights = [w / total for w in weights]
    row = lax.broadcasted_iota(jnp.int32, (HEAD_DIM, HEAD_DIM), 0)
    table = jnp.zeros((HEAD_DIM, HEAD_DIM), F32)
    for i, w in enumerate(weights):
        table = jnp.where(row == i, w, table)
    table = table.T
    between()
    sums = jnp.zeros((EACH, HEAD_DIM), F32)
    for i, part in enumerate(parts):
        sums += table[:EACH, i : i + 1] * part[:EACH].astype(F32)
    sums = sums.astype(BF)
    for at in range(out.shape[0]):
        out[at, :EACH] = sums
    if not finish:
        lines = lay_out((high, *split(total)))
        for at in range(out.shape[0]):
            out[at, EACH:] = lines


def combine(parts, copies, finish, name, *after):
    return pl.pallas_call(
        functools.partial(combine_kernel, len(parts)),
        in_specs=[WHOLE] * len(parts) + [ANY] * len(after),
        out_specs=WHOLE,
        out_shape=jax.ShapeDtypeStruct((copies, EACH if finish else SLOT, HEAD_DIM), BF),
        cost_estimate=pl.CostEstimate(
            flops=10**9, bytes_accessed=1 << 20, transcendentals=0
        ),
        compiler_params=pltpu.CompilerParams(vmem_limit_bytes=16 << 20),
        name=name,
    )(*parts, *after)


def halves_kernel(low, high, after, low_out, high_out, held, sems):
    half = low_out.shape[0]
    inward = [
        pltpu.make_async_copy(ref, held.at[i], sems.at[0, i])
        for i, ref in enumerate((low.at[0:half], high.at[half : 2 * half]))
    ]
    onward = [
        pltpu.make_async_copy(held.at[i], out, sems.at[1, i])
        for i, out in enumerate((low_out, high_out))
    ]
    for copy in inward:
        copy.start()
    for copy, following in zip(inward, onward):
        copy.wait()
        following.start()
    wait_all(onward)


def halves(low, high, after):
    shape = (low.shape[0] // 2, low.shape[1])
    return pl.pallas_call(
        halves_kernel,
        in_specs=[ANY] * 3,
        out_specs=(ANY, ANY),
        out_shape=[jax.ShapeDtypeStruct(shape, BF)] * 2,
        scratch_shapes=[pltpu.VMEM((2, *shape), BF), pltpu.SemaphoreType.DMA((2, 2))],
        cost_estimate=pl.CostEstimate(flops=0, bytes_accessed=2 << 20, transcendentals=0),
        compiler_params=pltpu.CompilerParams(vmem_limit_bytes=16 << 20),
        name="halves",
    )(low, high, after)


def video_kernel(pos, mask, valid, *rest):
    far, out_h, near, out, bias_s, sems = rest[:8], rest[9], rest[10:18], *rest[18:]
    q, tk, tv, own, z_low, z_high, t_low, t_high = near
    pairs = list(zip(far, near))
    begun = fetch(pairs, sems.at[0], FIRST)
    later = fetch(pairs, sems.at[1], REST)
    fill_bias(pos, mask, bias_s)
    text_bias = jnp.where(valid[...] > 0, 0.0, LOW)
    for head in range(HEADS_HERE):
        if head == 0:
            wait_all(begun)
        elif head == 1:
            wait_all(later)
        cols = slice(head * HEAD_DIM, (head + 1) * HEAD_DIM)
        one_head(
            q.at[:, cols],
            tk.at[:, cols],
            tv.at[:, cols],
            [ref.at[:, :, cols] for ref in (z_low, own, z_high)],
            [ref.at[:, :, :, cols] for ref in (t_low, t_high)],
            text_bias,
            bias_s,
            out.at[:, cols],
        )
    copy = pltpu.make_async_copy(out, out_h, sems.at[0, 0])
    copy.start()
    copy.wait()


def fill_bias(pos, mask, bias_s):
    row = lax.broadcasted_iota(jnp.int32, (8, PAIR), 0)
    col = lax.broadcasted_iota(jnp.int32, (8, PAIR), 1)
    second_q = row >= TILE
    second_k = jnp.bitwise_and(col, 7) >= TILE
    for a in range(2):
        for i in range(3):
            for j in range(3):
                where_t = pos[0] * 2 + a + i - 1
                where_h = pos[1] + j - 1
                inside = (where_t >= 0) & (where_t < pos[3]) & (where_h >= 0) & (where_h < pos[4])
                base = 9 * i + 3 * j

                def one(c, k):
                    if base + k == 13:
                        return jnp.where(inside, 0.0, LOW)
                    ok = inside & (mask[(a * 2 + c) * 27 + base + k] > 0)
                    return jnp.where(ok, 0.0, LOW)

                low = jnp.where(second_k, one(0, 2), one(0, 1))
                high = jnp.where(second_k, one(1, 1), one(1, 0))
                bias_s[a, i, j] = jnp.where(second_q, high, low)


def one_head(q, tk, tv, mids, sides, text_bias, bias_s, out):
    def rows(part):
        return (
            jnp.concatenate([sides[0][j, part] for j in range(3)], axis=0),
            jnp.concatenate(
                [ref[part, a * PAIR : (a + 1) * PAIR, :] for a in range(2) for ref in mids],
                axis=0,
            ),
            jnp.concatenate([sides[1][j, part] for j in range(3)], axis=0),
        )

    queries = q[...]
    k_low, k_mid, k_high = rows(0)
    v_low, v_mid, v_high = rows(1)
    s_mid = dot_t(queries, k_mid)
    s_text = dot_t(queries, tk[...])
    s_sides = (dot_t(queries[:PAIR], k_low), dot_t(queries[PAIR:], k_high))
    v_sides = (v_low, v_high)
    for a in range(2):
        mine = slice(a * PAIR, (a + 1) * PAIR)
        pieces = []
        for i in range(3):
            for j in range(3):
                at = (a + i - 1) * 3 + j
                if 0 <= a + i - 1 <= 1:
                    piece = s_mid[mine, at * PAIR : (at + 1) * PAIR]
                else:
                    piece = s_sides[a][:, j * PAIR : (j + 1) * PAIR]
                piece = piece.reshape(PAIR // 8, 8, PAIR) * SCALE2 + bias_s[a, i, j][None]
                pieces.append(piece.reshape(PAIR, PAIR))
        text_piece = s_text[mine] * SCALE2 + text_bias
        pieces.append(text_piece[:, :PAIR])
        pieces.append(text_piece[:, PAIR:])
        high = functools.reduce(jnp.maximum, pieces)
        high = jnp.max(high, axis=1, keepdims=True)
        weights = [jnp.exp2(piece - high) for piece in pieces]
        total = jnp.sum(functools.reduce(jnp.add, weights), axis=1, keepdims=True)
        weights = [w.astype(BF) for w in weights]
        side = weights[:3] if a == 0 else weights[6:9]
        mid = weights[3:9] if a == 0 else weights[:6]
        mixed = (
            dot(jnp.concatenate(side, axis=1), v_sides[a])
            + dot(jnp.concatenate(mid, axis=1), v_mid)
            + dot(jnp.concatenate(weights[9:], axis=1), tv[...])
        )
        out[mine, :] = (mixed / total).astype(BF)


def video_attention(pos, mask, valid, *arrays):
    return pl.pallas_call(
        video_kernel,
        in_specs=[SCALARS, SCALARS, WHOLE] + [FAR] * 4 + [ANY] * (len(arrays) - 4),
        out_specs=FAR,
        out_shape=jax.ShapeDtypeStruct((OWN, WIDTH), BF),
        scratch_shapes=[pltpu.VMEM(x.shape, BF) for x in arrays[:8]]
        + [pltpu.VMEM((OWN, WIDTH), BF), pltpu.VMEM((2, 3, 3, 8, PAIR), F32), pltpu.SemaphoreType.DMA((2, 8))],
        cost_estimate=pl.CostEstimate(
            flops=9 * 10**9, bytes_accessed=6 << 20, transcendentals=2 * 10**6
        ),
        compiler_params=pltpu.CompilerParams(vmem_limit_bytes=VMEM),
        name="video_attention",
    )(pos, mask, valid, *arrays)


def project(pos, near, mine, held, sems, read, put, out, sent, out_sems):
    width = held.shape[1] // 4
    for step, ref in zip((0, 1, 2, 3, 5, 6, 7), near):
        column = jnp.bitwise_and(pos[1] + step, 7)
        is_mine = lax.shift_right_logical(column, 2) == pos[2]
        slot = jnp.bitwise_and(column, 3)
        columns = pl.ds(pl.multiple_of(slot * width, width), width)

        @pl.when(is_mine if mine else jnp.logical_not(is_mine))
        def _():
            pltpu.make_async_copy(ref, held.at[:, columns], sems.at[slot]).start()

    column = jnp.bitwise_and(pos[1] + 4, 7)
    is_mine = lax.shift_right_logical(column, 2) == pos[2]
    late = is_mine if mine else jnp.logical_not(is_mine)
    late_slot = jnp.bitwise_and(column, 3)
    left = read()
    copies = []
    for pair in range(2):
        for slot in (2 * pair, 2 * pair + 1):
            columns = slice(slot * width, (slot + 1) * width)

            @pl.when(jnp.logical_not(late & (late_slot == slot)))
            def _():
                pltpu.make_async_copy(near[0], held.at[:, columns], sems.at[slot]).wait()

        columns = slice(2 * pair * width, 2 * (pair + 1) * width)
        sent[:, columns] = put(columns, dot(left, held[:, columns])).astype(BF)
        copies.append(
            pltpu.make_async_copy(sent.at[:, columns], out.at[:, columns], out_sems.at[pair])
        )
        copies[-1].start()
    wait_all(copies)


def by_head(parts):
    flat = parts.reshape(HEADS_HERE * TEXT, HEAD_DIM)
    heads = [flat[head * TEXT : (head + 1) * TEXT] for head in range(HEADS_HERE)]
    return jnp.concatenate(heads, axis=1)


def text_share_kernel(pos, parts_h, *rest):
    blocks, (video_h, top_h, bottom_h), rest = rest[:7], rest[7:10], rest[10:]
    rows_h, share, terms, far_share, parts, rows, video, w, far_sems, in_sems, *others = rest
    half = top_h.shape[0]
    rows_copy = pltpu.make_async_copy(rows, rows_h, in_sems.at[1])
    copy = pltpu.make_async_copy(parts_h, parts, in_sems.at[0])
    copy.start()
    copies = [
        pltpu.make_async_copy(video_h, video, far_sems.at[0]),
        pltpu.make_async_copy(top_h, w.at[0:half], far_sems.at[1]),
        pltpu.make_async_copy(bottom_h, w.at[half : 2 * half], far_sems.at[2]),
    ]
    for each in copies:
        each.start()

    def read():
        copy.wait()
        rows[...] = by_head(parts[...])
        rows_copy.start()
        wait_all(copies)
        for at, left in enumerate((video, rows)):
            part = slice(at * OWN, (at + 1) * OWN)
            terms[part, :] = dot(left[...], w[...])
            far_share[part, :] = terms[part, :].astype(BF)
        return rows[...]

    held, sent, sems, out_sems = others
    project(pos, blocks, False, held, sems, read, lambda _, x: x, share, sent, out_sems)
    rows_copy.wait()


def share_kernel(pos, rows_h, *rest):
    blocks, rest = rest[:7], rest[7:]
    share, rows, in_sems, held, sent, sems, out_sems = rest
    copy = pltpu.make_async_copy(rows_h, rows, in_sems.at[0])
    copy.start()

    def read():
        copy.wait()
        return rows[...]

    project(pos, blocks, False, held, sems, read, lambda _, x: x, share, sent, out_sems)


def finish_kernel(pos, rows_h, other_h, *rest):
    blocks, rest = rest[:7], rest[7:]
    out, rows, other, in_sems, held, sent, sems, out_sems = rest
    copies = [
        pltpu.make_async_copy(rows_h, rows, in_sems.at[0]),
        pltpu.make_async_copy(other_h, other, in_sems.at[1]),
    ]
    for copy in copies:
        copy.start()

    def read():
        wait_all(copies)
        return rows[...]

    def put(columns, terms):
        return terms + other[:, columns].astype(F32)

    project(pos, blocks, True, held, sems, read, put, out, sent, out_sems)


def project_call(kernel, name, pos, left, blocks, out_shape, out_specs, scratch, after=(), aliases=None):
    depth, width = blocks[0].shape
    return pl.pallas_call(
        kernel,
        in_specs=[SCALARS] + [FAR] + [ANY] * (len(left) - 1) + [ANY] * 7 + [ANY] * len(after),
        out_specs=out_specs,
        out_shape=out_shape,
        input_output_aliases=aliases or {},
        scratch_shapes=[pltpu.VMEM(x.shape, BF) for x in left]
        + scratch
        + [
            pltpu.SemaphoreType.DMA((2,)),
            pltpu.VMEM((depth, 4 * width), BF),
            pltpu.VMEM((TEXT, 4 * width), BF),
            pltpu.SemaphoreType.DMA((4,)),
            pltpu.SemaphoreType.DMA((2,)),
        ],
        cost_estimate=pl.CostEstimate(
            flops=8 * TEXT * depth * width, bytes_accessed=4 << 20, transcendentals=0
        ),
        compiler_params=pltpu.CompilerParams(vmem_limit_bytes=24 << 20),
        name=name,
    )(pos, *left, *blocks, *after)


def text_finish_kernel(pos, rows_h, other_h, *rest):
    blocks, (terms_h, far_h, _, out, video), rest = rest[:7], rest[7:12], rest[12:]
    rows, other, terms, far, done, far_sems, *others = rest
    width = terms.shape[1]
    column = jnp.bitwise_and(pos[1] + 4, 7)
    columns = pl.ds(pl.multiple_of(jnp.bitwise_and(column, 3) * width, width), width)
    is_mine = lax.shift_right_logical(column, 2) == pos[2]
    inward = [
        pltpu.make_async_copy(terms_h, terms, far_sems.at[0]),
        pltpu.make_async_copy(far_h, far, far_sems.at[1]),
    ]
    outward = [
        pltpu.make_async_copy(done.at[0:OWN], video.at[:, columns], far_sems.at[2]),
        pltpu.make_async_copy(done.at[OWN : OWN + TEXT], out.at[:, columns], far_sems.at[3]),
    ]

    @pl.when(is_mine)
    def _():
        for copy in inward:
            copy.start()

    finish_kernel(pos, rows_h, other_h, *blocks, out, rows, other, *others)

    @pl.when(is_mine)
    def _():
        wait_all(inward)
        done[...] = (terms[...] + far[...].astype(F32)).astype(BF)
        for copy in outward:
            copy.start()
        wait_all(outward)


def shards(video_q, video_kv, text_q, text_k, text_v, tile_mask, text_valid, w_out):
    frames, rows, cols, width = video_q.shape
    t_count, h_count = lax.axis_size("tm"), lax.axis_size("height")
    zero = jnp.int32(0)
    pos = jnp.stack(
        [
            lax.axis_index("tm"),
            lax.axis_index("height"),
            lax.axis_index("head"),
            zero + t_count * 2,
            zero + h_count,
        ]
    ).astype(jnp.int32)
    mask = tile_mask.reshape(-1)
    valid = text_valid.reshape(1, TEXT)
    own = video_kv.reshape(2, OWN, width)
    q = video_q.reshape(OWN, width)

    def up(x, axis, by=1):
        n = lax.axis_size(axis)
        return lax.ppermute(x, axis, [(i, (i + by) % n) for i in range(n)])

    def down(x, axis, by=1):
        return up(x, axis, -by)

    z_low, z_high = up(own, "height"), down(own, "height")
    parts, ring = text_part(pos, valid, text_q, own, text_k, text_v, w_out)
    before, after = [up(ring, "height")], [down(ring, "height")]
    parts = lax.all_to_all(parts, "tm", 0, 0, tiled=True)
    parts, low, high = merge(parts, h_count, own, z_low, z_high)
    t_low, t_high = up(low, "tm"), down(high, "tm")

    parts = lax.all_to_all(parts, "height", 0, 0, tiled=True)
    low, high = before[0], after[0]
    before.append(up(low, "height"))
    after.append(down(high, "height"))
    sums = combine([parts], t_count, True, "text_finish_sums")
    parts = lax.all_to_all(sums, "tm", 0, 0, tiled=True)
    low, high = before[1], after[1]
    before.append(up(low, "height"))
    after.append(down(high, "height"))
    video_rows = video_attention(
        pos, mask, valid, q, text_k, text_v, own, z_low, z_high, t_low, t_high, parts
    )
    low, high = halves(before[2], after[2], video_rows)
    far = [up(low, "height"), down(high, "height")]

    def swap(x):
        return lax.ppermute(x, "head", [(0, 1), (1, 0)])

    blocks = [w_out] + after + before[::-1]
    full = jax.ShapeDtypeStruct((OWN, 4 * w_out.shape[1]), BF)
    video_other = swap(
        project_call(share_kernel, "video_share", pos, [video_rows], blocks, full, FAR, [])
    )
    far_shape = (OWN + TEXT, w_out.shape[1])
    text_rows, text_other, terms, share = project_call(
        text_share_kernel,
        "text_share",
        pos,
        [parts],
        blocks,
        (
            jax.ShapeDtypeStruct((TEXT, WIDTH), BF),
            full,
            jax.ShapeDtypeStruct(far_shape, F32),
            jax.ShapeDtypeStruct(far_shape, BF),
        ),
        (FAR, FAR, WHOLE, WHOLE),
        [
            pltpu.VMEM((TEXT, WIDTH), BF),
            pltpu.VMEM((OWN, WIDTH), BF),
            pltpu.VMEM(w_out.shape, BF),
            pltpu.SemaphoreType.DMA((3,)),
        ],
        [video_rows, *far],
    )
    text_other = swap(text_other)
    video_out = project_call(
        finish_kernel, "video_finish", pos, [video_rows, video_other], blocks, full, FAR, []
    )
    text_out, video_out = project_call(
        text_finish_kernel,
        "text_finish",
        pos,
        [text_rows, text_other],
        blocks,
        (full, full),
        (FAR, ANY),
        [pltpu.VMEM(terms.shape, t) for t in (F32, BF, BF)] + [pltpu.SemaphoreType.DMA((4,))],
        [terms, swap(share), video_out],
        {12: 1},
    )
    return video_out.reshape(frames, rows, cols, -1), text_out


def solution(mesh):
    return jax.shard_map(
        shards,
        mesh=mesh,
        in_specs=(
            P("tm", "height", None, "head"),
            P(None, "tm", "height", None, "head"),
            P(None, "head"),
            P(None, "head"),
            P(None, "head"),
            P("tm", "height", None, None),
            P(),
            P("head", "height"),
        ),
        out_specs=(P("tm", "height", None, "head"), P(None, "head")),
        check_vma=False,
    )
```
